128 devices in a mesh: group: 8 (over y, core), dev: 16 (over z, x).
Axes of the slice: x: 4, y: 4, z: 4, core: 2. Of those that a mesh axis runs over, the one named last changes fastest.
Arguments:
- embeds: bfloat16 [49152, 1024], P(('group', 'dev')), may hold values from -30 to 30, as said below
- cluster_id: int32 [49152], P(('group', 'dev')), may hold values from 0 to 23, as said below
- owner_slot: int32 [24], replicated, may hold values from 0 to 23, each once
Outputs:
- near_max: float32 [8, 16, 3, 256], P('group', 'dev')
- neighbor_logsumexp: float32 [8, 16, 3, 256], P('group', 'dev')
The draws below stay inside these ranges and needn't reach their ends.
Inputs may be any that keep to these rules, and one draw needn't show every extreme that they name: `cluster_id`: at most 32 rows of one device name the same cluster, and every cluster is named by two or more rows. owner_slot[c] = 3 * g + l: group g owns cluster c as its l-th cluster. `embeds`: every row has a sum of squares over its 1024 features of 1 or more.
All inputs are finite; a program needn't handle non-finite values.
Results may differ from the reference program's by a relative error of at most 0.00042.
Values may be sent and summed in bfloat16 or wider, within the bound.
A program may use at most 128 MiB of HBM per device.

```python
import jax
import jax.numpy as jnp
from jax import lax

D = 1024
ROWS_DEV = 384
CL_GROUP = 3
NCLUST = 24
MOST = 32
SLOTS = 256
GROUP_DEVS = 16
N_ROWS = 49152
N_GROUP = 8
N_DEV = 16


def draw_embeds(key, part):
    key = jax.random.fold_in(key, 5)
    key_base, key_dir, key_pick, key_coef = jax.random.split(key, 4)
    base = jax.random.normal(key_base, (N_ROWS, D), jnp.float32)
    coef = jnp.exp(jax.random.uniform(key_coef, (N_ROWS,), jnp.float32, jnp.log(0.2), jnp.log(3.0)))
    direction = jax.random.normal(key_dir, (64, D), jnp.float32)
    picked = jax.random.randint(key_pick, (N_ROWS,), 0, 64)
    values = base + coef[:, None] * direction[picked]
    return jnp.clip(values, -30.0, 30.0).astype(jnp.bfloat16)


def draw_cluster_id(key, part):
    key = jax.random.fold_in(key, 11)
    key_power, key_noise, key_offset, key_order = jax.random.split(key, 4)
    blocks = N_ROWS // ROWS_DEV
    labels = NCLUST * MOST
    power = jax.random.randint(key_power, (NCLUST,), 0, 5)
    weight = jnp.left_shift(jnp.ones((NCLUST,), jnp.int32), power)
    label_index = jnp.arange(labels, dtype=jnp.int32)
    cluster = label_index // MOST
    ranking = label_index % MOST
    noise = jax.random.randint(key_noise, (blocks, labels), 0, 65536)
    score = noise * weight[cluster][None, :] * labels + label_index[None, :]
    offset = jax.random.randint(key_offset, (), 0, NCLUST)
    block_index = jnp.arange(blocks, dtype=jnp.int32)
    filled = (block_index % GROUP_DEVS + offset) % NCLUST
    single = block_index % NCLUST
    forced = (cluster[None, :] == filled[:, None]) | (cluster[None, :] == single[:, None]) & (ranking[None, :] == 0)
    score = score + jnp.where(forced, 1073741824, 0)
    chosen = lax.top_k(score, ROWS_DEV)[1]
    order_keys = jax.random.split(key_order, blocks)
    shuffled = jax.vmap(lambda one_key, picked: jax.random.permutation(one_key, picked))(order_keys, chosen)
    return (shuffled // MOST).reshape(-1).astype(jnp.int32)


def setup_inputs(seed: int = 0) -> dict:
    key_of = jax.random.split(jax.random.key(seed), 4)
    embeds = draw_embeds(jax.random.fold_in(key_of[3], 71), 0)
    cluster_id = draw_cluster_id(jax.random.fold_in(key_of[3], 71), 0)
    owner_slot = jax.random.permutation(key_of[2], NCLUST).astype(jnp.int32)
    return {"embeds": embeds, "cluster_id": cluster_id, "owner_slot": owner_slot}


SOFTMAX_TEMPER = 0.05
EPSILON = 1e-06
FLOOR = -2.0
LIVE_LEVEL = -1.5

def unit_rows(embeds):
    widened = embeds.astype(jnp.float32)
    scale = lax.rsqrt(lax.optimization_barrier(jnp.sum(widened * widened, axis=1, keepdims=True)) + EPSILON)
    return (widened * scale).astype(jnp.bfloat16)

def cluster_stats(packed):
    members, present_flags = packed
    widened = members.astype(jnp.float32)
    similarity_scores = jnp.dot(widened, widened.T, precision=lax.Precision.HIGHEST)
    extent = members.shape[0]
    retained_rows = (present_flags[None, :] > 0.5) & (jnp.arange(extent)[:, None] != jnp.arange(extent)[None, :])
    highest = lax.optimization_barrier(jnp.max(jnp.where(retained_rows, similarity_scores, FLOOR), axis=1))
    summed_terms = lax.optimization_barrier(jnp.sum(jnp.where(retained_rows, jnp.exp((similarity_scores - highest[:, None]) / SOFTMAX_TEMPER), 0.0), axis=1))
    has_other = (present_flags > 0.5) & (highest > LIVE_LEVEL)
    near_max = jnp.where(present_flags > 0.5, highest, 0.0)
    neighbor_logsumexp = jnp.where(has_other, highest / SOFTMAX_TEMPER + jnp.log(jnp.where(has_other, summed_terms, 1.0)), 0.0)
    return (near_max, neighbor_logsumexp)

def to_owner_layout(values, owner_slot):
    shaped = values.reshape(NCLUST, N_GROUP, N_DEV, MOST).transpose(0, 2, 1, 3).reshape(NCLUST, N_DEV, SLOTS)
    placed = jnp.zeros_like(shaped).at[owner_slot].set(shaped)
    return placed.reshape(N_GROUP, CL_GROUP, N_DEV, SLOTS).transpose(0, 2, 1, 3)

def reference(embeds, cluster_id, owner_slot):
    blocks = N_ROWS // ROWS_DEV
    capacity = blocks * MOST
    unit = unit_rows(embeds)
    labels = cluster_id.reshape(blocks, ROWS_DEV)
    onehot = (labels[:, :, None] == jnp.arange(NCLUST, dtype=jnp.int32)[None, None, :]).astype(jnp.int32)
    ranking = lax.optimization_barrier(jnp.sum((jnp.cumsum(onehot, axis=1) - 1) * onehot, axis=2))
    device = jnp.arange(blocks, dtype=jnp.int32)[:, None]
    position = (labels * capacity + device * MOST + ranking).reshape(-1).astype(jnp.int32)
    padded = jnp.zeros((NCLUST * capacity, D), jnp.bfloat16).at[position].set(unit)
    present_flags = jnp.zeros((NCLUST * capacity,), jnp.float32).at[position].set(1.0)
    near_max, neighbor_logsumexp = lax.map(cluster_stats, (padded.reshape(NCLUST, capacity, D), present_flags.reshape(NCLUST, capacity)))
    return (to_owner_layout(near_max, owner_slot), to_owner_layout(neighbor_logsumexp, owner_slot))
```

```python
import functools
import math

import jax
import jax.numpy as jnp
from jax import lax
from jax.experimental import pallas as pl
from jax.experimental.pallas import tpu as pltpu
from jax.sharding import PartitionSpec as P

MESH = pl.DeviceIdType.MESH
SHARP = 20.0 * math.log2(math.e)
ABSENT = -1e30
COLS = ((0, 384), (384, 768), (768, 1024))
HALVES = 2


def mod4(value):
    return lax.rem(value + 16, 4)


def place():
    g = lax.axis_index("group")
    d = lax.axis_index("dev")
    return lax.rem(d, 4), g // 2, d // 4, lax.rem(g, 2)


def device(x, y, z, core):
    return (y * 2 + core, z * 4 + x)


def root_of(g, l):
    y = g // 2
    if l < 2:
        x = lax.rem(g, 2) * 2 + l
        return x, y, mod4(x + y)
    x = mod4(y - lax.rem(g, 2))
    return x, y, mod4(x + y + 2)


def slot_positions(own):
    g = (own * 11) >> 5
    l = own - 3 * g
    y = g >> 1
    odd = g & 1
    second = l == 2
    x = jnp.where(second, (y - odd) & 3, odd * 2 + l)
    z = jnp.where(second, x + y + 2, x + y) & 3
    return (
        x * 6 + jnp.where(second, 4 + odd, y),
        y * 6 + jnp.where(second, 5 - odd, z),
        z * 6 + jnp.where(second, 4 + (x >> 1), x),
    )


class Order:
    def __init__(self, kind, x, y, z, core):
        self.kind = kind
        self.a, self.b, self.c = ((x, y, z), (y, z, x), (z, x, y))[kind]
        self.core = core

    def at(self, a, b, c):
        x, y, z = ((a, b, c), (c, a, b), (b, c, a))[self.kind]
        return device(x, y, z, self.core)

    def first(self, a, b):
        return mod4((a + b, b - a, a - b)[self.kind])

    def has_second(self, a, b):
        if self.kind == 0:
            return mod4(b - a) < 2
        if self.kind == 1:
            return mod4(b - 2 * a - 1) < 2
        return (a < 2) == (lax.rem(b, 2) == 1)

    def second_slot(self, a, b):
        return 4 + (mod4(b - a), mod4(b - 2 * a - 1), b // 2)[self.kind]


def kernel(
    embeds, cid, owner, near_out, lse_out,
    raw, unit, pk0, pk1, pk2, ra0, ra1, ra2, rb0, rb1, rb2, rows, bias, flags, high, total, stats, landed,
    in_sem, s1, r1, c1, s2, r2, c2, s3, r3, c3, sx, rx, so, ro, co,
):
    x, y, z, core = place()
    pk, ra, rb = (pk0, pk1, pk2), (ra0, ra1, ra2), (rb0, rb1, rb2)
    orders = [Order(kind, x, y, z, core) for kind in range(3)]
    is_first = z == mod4(x + y)
    is_second = (z == mod4(x + y + 2)) & (mod4(y - x) < 2)
    is_root = is_first | is_second
    root_g = jnp.where(is_first, 2 * y + x // 2, 2 * y + mod4(y - x))
    root_l = jnp.where(is_first, lax.rem(x, 2), 2)
    peer = device(x, y, z, 1 - core)

    fetch = pltpu.make_async_copy(embeds, raw, in_sem)
    fetch.start()

    barrier = pltpu.get_barrier_semaphore()

    def greet(target):
        pl.semaphore_signal(barrier, inc=1, device_id=target, device_id_type=MESH)

    for step in (1, 2, 3):
        greet(device(mod4(x + step), y, z, core))
        greet(device(x, mod4(y + step), z, core))
        greet(device(x, y, mod4(z + step), core))
    greet(peer)
    g = lax.axis_index("group")
    for l in range(3):
        qx, qy, qz = root_of(g, l)
        for k in range(2):
            @pl.when((qx != x) | (qy != y) | (qz != z) | (core != k))
            def _():
                greet(device(qx, qy, qz, k))

    n = raw.shape[0]
    ids = cid[...]
    own = jnp.zeros_like(ids)
    for c in range(24):
        own = jnp.where(ids == c, owner[c], own)
    member = (lax.broadcasted_iota(jnp.int32, (32, n), 0) == ids).astype(jnp.float32)
    earlier = lax.broadcasted_iota(jnp.int32, (n, n), 0) < lax.broadcasted_iota(jnp.int32, (n, n), 1)
    before = jnp.dot(
        member.astype(jnp.bfloat16), earlier.astype(jnp.float32).astype(jnp.bfloat16), preferred_element_type=jnp.float32
    )
    rank = jnp.sum(member * before, axis=0, keepdims=True).astype(jnp.int32)
    spots = [slot * 16 + (rank & 15) + (rank >> 4) * 384 for slot in slot_positions(own)]

    fetch.wait()
    wide = raw[...].astype(jnp.float32)
    scale = lax.rsqrt(jnp.sum(wide * wide, axis=1, keepdims=True) + 1e-6)
    unit[...] = (wide * scale).astype(jnp.bfloat16)

    targets = lax.broadcasted_iota(jnp.int32, (384, n), 0)
    for half in range(HALVES):
        for kind, (lo, hi) in enumerate(COLS):
            pick = (targets == spots[kind] - half * 384).astype(jnp.float32).astype(jnp.bfloat16)
            moved = jnp.dot(pick, unit[:, lo:hi], preferred_element_type=jnp.float32)
            pk[kind][half] = moved.astype(jnp.bfloat16).reshape(4, 6, 16, hi - lo)

    extra = jnp.where(core == lax.rem(root_g, 2), 15, 16)
    pl.semaphore_wait(barrier, 10 + jnp.where(is_root, extra, 0))

    def remote(src, dst, send, recv, target):
        return pltpu.make_async_remote_copy(
            src_ref=src, dst_ref=dst, send_sem=send, recv_sem=recv, device_id=target, device_id_type=MESH
        )

    def drain(ref, sem):
        pltpu.make_async_copy(ref, ref, sem).wait()

    for half in range(HALVES):
        for kind, order in enumerate(orders):
            a, b, c = order.a, order.b, order.c
            for step in (1, 2, 3):
                to = mod4(a + step)
                remote(
                    pk[kind].at[half, to], ra[kind].at[half, a], s1.at[kind, half], r1.at[kind, half], order.at(to, b, c)
                ).start()
            pltpu.make_async_copy(pk[kind].at[half, a], ra[kind].at[half, a], c1.at[kind, half]).start()

    def landing(kind, which, half, b):
        return rb[kind].at[which, half, :, b] if kind == 2 else rb[kind].at[which, half, b]

    for half in range(HALVES):
        for kind, order in enumerate(orders):
            a, b, c = order.a, order.b, order.c
            drain(ra[kind].at[half, pl.ds(0, 3)], r1.at[kind, half])
            drain(ra[kind].at[half, 0], c1.at[kind, half])
            for step in (1, 2, 3):
                to = mod4(b + step)
                remote(
                    ra[kind].at[half, :, to], landing(kind, 0, half, b),
                    s2.at[kind, half, 0], r2.at[kind, half, 0], order.at(a, to, c),
                ).start()

                @pl.when(order.has_second(a, to))
                def _():
                    remote(
                        ra[kind].at[half, :, order.second_slot(a, to)], landing(kind, 1, half, b),
                        s2.at[kind, half, 1], r2.at[kind, half, 1], order.at(a, to, c),
                    ).start()

            pltpu.make_async_copy(ra[kind].at[half, :, b], landing(kind, 0, half, b), c2.at[kind, half, 0]).start()

            @pl.when(order.has_second(a, b))
            def _():
                pltpu.make_async_copy(
                    ra[kind].at[half, :, order.second_slot(a, b)], landing(kind, 1, half, b), c2.at[kind, half, 1]
                ).start()

    def final(kind, half, c):
        lo, hi = COLS[kind]
        if kind == 0:
            return rows.at[0, half, c, :, :, :, pl.ds(lo, hi - lo)]
        if kind == 1:
            return rows.at[0, half, :, :, c, :, pl.ds(lo, hi - lo)]
        return rows.at[0, half, :, c, :, :, pl.ds(lo, hi - lo)]

    for half in range(HALVES):
        for kind, order in enumerate(orders):
            a, b, c = order.a, order.b, order.c

            def pass_on(which):
                drain(rb[kind].at[which, half, pl.ds(0, 3)], r2.at[kind, half, which])
                drain(rb[kind].at[which, half, 0], c2.at[kind, half, which])
                to = mod4(order.first(a, b) + 2 * which)

                @pl.when(c != to)
                def _():
                    remote(
                        rb[kind].at[which, half], final(kind, half, c), s3.at[kind, half, which], r3.at[kind, half],
                        order.at(a, b, to),
                    ).start()

                @pl.when(c == to)
                def _():
                    pltpu.make_async_copy(rb[kind].at[which, half], final(kind, half, c), c3.at[kind, half]).start()

            pass_on(0)

            @pl.when(order.has_second(a, b))
            def _():
                pass_on(1)

    eye = lax.broadcasted_iota(jnp.int32, (256, 256), 0) == lax.broadcasted_iota(jnp.int32, (256, 256), 1)

    def block(which, half, part):
        return rows[which, half, part].reshape(256, 1024)

    def scores(left, right):
        return lax.dot_general(left, right, (((1,), (1,)), ((), ())), preferred_element_type=jnp.float32)

    def gather(values, half, part):
        shaped = values.reshape(32, 8, 256)
        high[half, part] = jnp.maximum(high[half, part], jnp.max(shaped, axis=0))
        total[half, part] = total[half, part] + jnp.sum(jnp.exp2(shaped), axis=0)

    def prepare(which, half):
        @pl.loop(0, 4)
        def _(part):
            me = block(which, half, part)
            score = scores(me, me)
            own_score = jnp.where(eye, score, 0.0)
            there = jnp.where(jnp.sum(own_score, axis=1, keepdims=True) > 0.5, -SHARP, ABSENT)
            spread = jnp.broadcast_to(there, (256, 256))
            bias[which, half, part] = spread
            if which == 0:
                flags[half, part] = jnp.sum(own_score.reshape(32, 8, 256), axis=0)
                gather(jnp.where(eye, ABSENT, score * SHARP + spread), half, part)

    def pairs(which, half, other):
        @pl.loop(0, 4)
        def _(part):
            left = block(which, half, part)
            spread = bias[which, half, part]

            def one(target):
                gather(scores(left, block(0, other, target)) * SHARP + spread, other, target)

            if which == 0 and half == other:
                for step in (1, 2, 3):
                    one(mod4(part + step))
            else:
                for target in range(4):
                    one(target)

    @pl.when(is_root)
    def _():
        high[...] = jnp.full(high.shape, ABSENT, jnp.float32)
        total[...] = jnp.zeros(total.shape, jnp.float32)
        for half in range(HALVES):
            for kind in range(3):
                drain(rb[kind].at[0, half, pl.ds(0, 3)], r3.at[kind, half]) if False else None
                lo, hi = COLS[kind]
                drain(rows.at[0, half, pl.ds(0, 3), :, :, :, pl.ds(lo, hi - lo)], r3.at[kind, half])
                drain(rows.at[0, half, 0, :, :, :, pl.ds(lo, hi - lo)], c3.at[kind, half])
            remote(rows.at[0, half], rows.at[1, half], sx.at[half], rx.at[half], peer).start()
            prepare(0, half)
            for other in range(half + 1):
                pairs(0, half, other)
                if other != half:
                    pairs(0, other, half)
            drain(rows.at[1, half], rx.at[half])
            prepare(1, half)
            for other in range(half + 1):
                pairs(1, half, other)
                if other != half:
                    pairs(1, other, half)
        for half in range(HALVES):
            for part in range(4):
                present = jnp.sum(flags[half, part], axis=0, keepdims=True) > 0.5
                top = jnp.max(high[half, part], axis=0, keepdims=True)
                mass = jnp.sum(total[half, part], axis=0, keepdims=True)
                paired = present & (top > 0.5 * ABSENT)
                near = jnp.where(paired, top * (1.0 / SHARP) + 1.0, -2.0)
                stats[part, half : half + 1] = jnp.where(present, near, 0.0)
                stats[part, 2 + half : 3 + half] = jnp.where(paired, 20.0 + jnp.log(jnp.where(paired, mass, 1.0)), 0.0)
        spot = root_l * 2 + core
        for part in range(4):
            for column in range(4):
                target = device(column, root_g // 2, part, lax.rem(root_g, 2))
                same = (x == column) & (z == part) & (core == lax.rem(root_g, 2))

                @pl.when(jnp.logical_not(same))
                def _():
                    remote(stats.at[part], landed.at[spot], so, ro, target).start()

                @pl.when(same)
                def _():
                    copy = pltpu.make_async_copy(stats.at[part], landed.at[spot], co)
                    copy.start()
                    copy.wait()

    in_mine = jnp.int32(0)
    for l in range(3):
        qx, qy, qz = root_of(g, l)
        in_mine = in_mine + jnp.where((qx == x) & (qy == y) & (qz == z), 1, 0)

    @pl.when(in_mine == 0)
    def _():
        drain(landed, ro)

    @pl.when(in_mine != 0)
    def _():
        drain(landed.at[pl.ds(0, 5)], ro)

    lane = lax.broadcasted_iota(jnp.int32, (8, 256), 1)
    keep = lax.rem(lane, 64) < 16
    for l in range(3):
        near = jnp.zeros((1, 256), jnp.float32)
        lse = jnp.zeros((1, 256), jnp.float32)
        for k in range(2):
            mine = jnp.where(keep, pltpu.roll(landed[2 * l + k], lax.rem(256 - 16 * x, 256), 1), 0.0)
            for half in range(HALVES):
                shift = k * 32 + half * 16
                moved = pltpu.roll(mine, shift, 1) if shift else mine
                near = near + moved[half : half + 1]
                lse = lse + moved[2 + half : 3 + half]
        near_out[l : l + 1] = near
        lse_out[l : l + 1] = lse

    for half in range(HALVES):
        for kind, order in enumerate(orders):
            a, b, c = order.a, order.b, order.c
            drain(pk[kind].at[half, pl.ds(0, 3)], s1.at[kind, half])
            drain(rb[kind].at[0, half, pl.ds(0, 3)], s2.at[kind, half, 0])
            for step in (1, 2, 3):
                @pl.when(order.has_second(a, mod4(b + step)))
                def _():
                    drain(rb[kind].at[1, half, 0], s2.at[kind, half, 1])

            @pl.when(c != order.first(a, b))
            def _():
                drain(rb[kind].at[0, half], s3.at[kind, half, 0])

            @pl.when(order.has_second(a, b) & (c != mod4(order.first(a, b) + 2)))
            def _():
                drain(rb[kind].at[1, half], s3.at[kind, half, 1])

    @pl.when(is_root)
    def _():
        for half in range(HALVES):
            drain(rows.at[0, half], sx.at[half])
        for count in range(15):
            drain(stats.at[0], so)

        @pl.when(core != lax.rem(root_g, 2))
        def _():
            drain(stats.at[0], so)


def solution(mesh):
    def step(embeds, cluster_id, owner_slot):
        n, width = embeds.shape
        bf, f32 = jnp.bfloat16, jnp.float32
        widths = [hi - lo for lo, hi in COLS]
        vmem = pltpu.VMEM
        dma = pltpu.SemaphoreType.DMA
        near, lse = pl.pallas_call(
            kernel,
            out_shape=[jax.ShapeDtypeStruct((3, 256), f32)] * 2,
            in_specs=[
                pl.BlockSpec(memory_space=pl.ANY),
                pl.BlockSpec(memory_space=pltpu.VMEM),
                pl.BlockSpec(memory_space=pltpu.SMEM),
            ],
            out_specs=[pl.BlockSpec(memory_space=pltpu.VMEM)] * 2,
            scratch_shapes=[vmem((n, width), bf), vmem((n, width), bf)]
            + [vmem((2, 4, 6, 16, w), bf) for w in widths]
            + [vmem((2, 4, 6, 16, w), bf) for w in widths]
            + [vmem((2, 2, 4, 4, 16, w), bf) for w in widths]
            + [
                vmem((2, 2, 4, 4, 4, 16, width), bf),
                vmem((2, 2, 4, 256, 256), f32),
                vmem((2, 4, 8, 256), f32),
                vmem((2, 4, 8, 256), f32),
                vmem((2, 4, 8, 256), f32),
                vmem((4, 8, 256), f32),
                vmem((6, 8, 256), f32),
                dma, dma((3, 2)), dma((3, 2)), dma((3, 2)),
                dma((3, 2, 2)), dma((3, 2, 2)), dma((3, 2, 2)),
                dma((3, 2, 2)), dma((3, 2)), dma((3, 2)),
                dma((2,)), dma((2,)), dma, dma, dma,
            ],
            compiler_params=pltpu.CompilerParams(
                collective_id=0, has_side_effects=True, vmem_limit_bytes=56 * 1024 * 1024
            ),
        )(embeds, cluster_id.reshape(1, n), owner_slot)
        return near[None, None], lse[None, None]

    return jax.shard_map(
        step,
        mesh=mesh,
        in_specs=(P(("group", "dev"), None), P(("group", "dev")), P()),
        out_specs=(P("group", "dev", None, None), P("group", "dev", None, None)),
        check_vma=False,
    )
```

```python
import functools
import math

import jax
import jax.numpy as jnp
from jax import lax
from jax.experimental import pallas as pl
from jax.experimental.pallas import tpu as pltpu
from jax.sharding import PartitionSpec as P

MESH = pl.DeviceIdType.MESH
SHARP = 20.0 * math.log2(math.e)
ABSENT = -1e30
COLS = ((0, 384), (384, 768), (768, 1024))
HALVES = 2


def mod4(value):
    return lax.rem(value + 16, 4)


def place():
    g = lax.axis_index("group")
    d = lax.axis_index("dev")
    return lax.rem(d, 4), g // 2, d // 4, lax.rem(g, 2)


def device(x, y, z, core):
    return (y * 2 + core, z * 4 + x)


def root_of(g, l):
    y = g // 2
    if l < 2:
        x = lax.rem(g, 2) * 2 + l
        return x, y, mod4(x + y)
    x = mod4(y - lax.rem(g, 2))
    return x, y, mod4(x + y + 2)


def slot_positions(own):
    g = (own * 11) >> 5
    l = own - 3 * g
    y = g >> 1
    odd = g & 1
    second = l == 2
    x = jnp.where(second, (y - odd) & 3, odd * 2 + l)
    z = jnp.where(second, x + y + 2, x + y) & 3
    return (
        x * 6 + jnp.where(second, 4 + odd, y),
        y * 6 + jnp.where(second, 5 - odd, z),
        z * 6 + jnp.where(second, 4 + (x >> 1), x),
    )


class Order:
    def __init__(self, kind, x, y, z, core):
        self.kind = kind
        self.a, self.b, self.c = ((x, y, z), (y, z, x), (z, x, y))[kind]
        self.core = core

    def at(self, a, b, c):
        x, y, z = ((a, b, c), (c, a, b), (b, c, a))[self.kind]
        return device(x, y, z, self.core)

    def first(self, a, b):
        return mod4((a + b, b - a, a - b)[self.kind])

    def has_second(self, a, b):
        if self.kind == 0:
            return mod4(b - a) < 2
        if self.kind == 1:
            return mod4(b - 2 * a - 1) < 2
        return (a < 2) == (lax.rem(b, 2) == 1)

    def second_slot(self, a, b):
        return 4 + (mod4(b - a), mod4(b - 2 * a - 1), b // 2)[self.kind]


def kernel(
    embeds, cid, owner, near_out, lse_out,
    raw, unit, pk0, pk1, pk2, ra0, ra1, ra2, rb0, rb1, rb2, rows, shade, veil, high, total, side_high, side_total,
    swap, swapped, stats, landed,
    in_sem, s1, r1, c1, s2, r2, c2, s3, r3, c3, sx, rx, se, re, so, ro, co,
):
    x, y, z, core = place()
    pk, ra, rb = (pk0, pk1, pk2), (ra0, ra1, ra2), (rb0, rb1, rb2)
    orders = [Order(kind, x, y, z, core) for kind in range(3)]
    is_first = z == mod4(x + y)
    is_second = (z == mod4(x + y + 2)) & (mod4(y - x) < 2)
    is_root = is_first | is_second
    root_g = jnp.where(is_first, 2 * y + x // 2, 2 * y + mod4(y - x))
    root_l = jnp.where(is_first, lax.rem(x, 2), 2)
    peer = device(x, y, z, 1 - core)
    g = lax.axis_index("group")

    fetch = pltpu.make_async_copy(embeds, raw, in_sem)
    fetch.start()

    barrier = pltpu.get_barrier_semaphore()

    def greet(target):
        pl.semaphore_signal(barrier, inc=1, device_id=target, device_id_type=MESH)

    for step in (1, 2, 3):
        greet(device(mod4(x + step), y, z, core))
        greet(device(x, mod4(y + step), z, core))
        greet(device(x, y, mod4(z + step), core))
    greet(peer)

    n = raw.shape[0]
    ids = cid[...].reshape(1, n)
    own = jnp.zeros_like(ids)
    for c in range(24):
        own = jnp.where(ids == c, owner[c], own)
    member = (lax.broadcasted_iota(jnp.int32, (32, n), 0) == ids).astype(jnp.float32)
    earlier = lax.broadcasted_iota(jnp.int32, (n, n), 0) < lax.broadcasted_iota(jnp.int32, (n, n), 1)
    before = jnp.dot(
        member.astype(jnp.bfloat16), earlier.astype(jnp.float32).astype(jnp.bfloat16), preferred_element_type=jnp.float32
    )
    rank = jnp.sum(member * before, axis=0, keepdims=True).astype(jnp.int32)
    spots = [slot * 16 + (rank & 15) + (rank >> 4) * 384 for slot in slot_positions(own)]

    fetch.wait()
    wide = raw[...].astype(jnp.float32)
    scale = lax.rsqrt(jnp.sum(wide * wide, axis=1, keepdims=True) + 1e-6)
    unit[...] = (wide * scale).astype(jnp.bfloat16)

    targets = lax.broadcasted_iota(jnp.int32, (384, n), 0)
    for half in range(HALVES):
        for kind, (lo, hi) in enumerate(COLS):
            pick = (targets == spots[kind] - half * 384).astype(jnp.float32).astype(jnp.bfloat16)
            moved = jnp.dot(pick, unit[:, lo:hi], preferred_element_type=jnp.float32)
            pk[kind][half] = moved.astype(jnp.bfloat16).reshape(4, 6, 16, hi - lo)

    @pl.when(is_root)
    def _():
        high[...] = jnp.full(high.shape, ABSENT, jnp.float32)
        total[...] = jnp.zeros(total.shape, jnp.float32)
        side_high[...] = jnp.full(side_high.shape, ABSENT, jnp.float32)
        side_total[...] = jnp.zeros(side_total.shape, jnp.float32)

    pl.semaphore_wait(barrier, 10)

    def remote(src, dst, send, recv, target):
        return pltpu.make_async_remote_copy(
            src_ref=src, dst_ref=dst, send_sem=send, recv_sem=recv, device_id=target, device_id_type=MESH
        )

    def drain(ref, sem):
        pltpu.make_async_copy(ref, ref, sem).wait()

    for half in range(HALVES):
        for kind, order in enumerate(orders):
            a, b, c = order.a, order.b, order.c
            for step in (1, 2, 3):
                to = mod4(a + step)
                remote(
                    pk[kind].at[half, to], ra[kind].at[half, a // 2, lax.rem(a, 2)],
                    s1.at[kind, half], r1.at[kind, half], order.at(to, b, c),
                ).start()
            pltpu.make_async_copy(
                pk[kind].at[half, a], ra[kind].at[half, a // 2, lax.rem(a, 2)], c1.at[kind, half]
            ).start()

    def landing(kind, which, half, b):
        if kind == 2:
            return rb[kind].at[which, half, :, :, b // 2, lax.rem(b, 2)]
        return rb[kind].at[which, half, b // 2, lax.rem(b, 2)]

    def second_phase(half):
        for kind, order in enumerate(orders):
            a, b, c = order.a, order.b, order.c
            drain(pk[kind].at[half, pl.ds(0, 3)], r1.at[kind, half])
            drain(pk[kind].at[half, 0], c1.at[kind, half])
            for step in (1, 2, 3):
                to = mod4(b + step)
                remote(
                    ra[kind].at[half, :, :, to], landing(kind, 0, half, b),
                    s2.at[kind, half, 0], r2.at[kind, half, 0], order.at(a, to, c),
                ).start()

                @pl.when(order.has_second(a, to))
                def _():
                    remote(
                        ra[kind].at[half, :, :, order.second_slot(a, to)], landing(kind, 1, half, b),
                        s2.at[kind, half, 1], r2.at[kind, half, 1], order.at(a, to, c),
                    ).start()

            pltpu.make_async_copy(ra[kind].at[half, :, :, b], landing(kind, 0, half, b), c2.at[kind, half, 0]).start()

            @pl.when(order.has_second(a, b))
            def _():
                pltpu.make_async_copy(
                    ra[kind].at[half, :, :, order.second_slot(a, b)], landing(kind, 1, half, b), c2.at[kind, half, 1]
                ).start()

    def piece(kind, which, q, low):
        lo, hi = COLS[kind]
        half, odd = q // 2, q % 2
        cols = pl.ds(lo, hi - lo)
        xl, yl, zl = lax.rem(x, 2), lax.rem(y, 2), lax.rem(z, 2)
        if kind == 0:
            other = lax.rem(odd + zl + low, 2)
            dst = rows.at[0, q, zl, low, z // 2, :, :, :, cols]
        elif kind == 1:
            other = lax.rem(odd + xl + low, 2)
            dst = rows.at[0, q, low, other, :, :, x // 2, :, cols]
        else:
            other = lax.rem(odd + yl + low, 2)
            dst = rows.at[0, q, low, yl, :, y // 2, :, :, cols]
        return rb[kind].at[which, half, :, low, :, other], dst

    def sends(kind, which):
        order = orders[kind]
        to = mod4(order.first(order.a, order.b) + 2 * which)
        return order.c != to, to

    def third_phase(q):
        half = q // 2
        for kind, order in enumerate(orders):
            a, b = order.a, order.b

            def pass_on(which):
                if q % 2 == 0:
                    drain(pk[kind].at[half, pl.ds(0, 2)], r2.at[kind, half, which])
                    drain(rb[kind].at[0, 0, 0, 0], c2.at[kind, half, which])
                away, to = sends(kind, which)

                @pl.when(away)
                def _():
                    if q:
                        @pl.when(jnp.logical_not(is_root))
                        def _():
                            drain(rb[kind].at[0, 0, 0], s3.at[kind, which, q - 1])


                    for low in range(2):
                        src, dst = piece(kind, which, q, low)
                        remote(src, dst, s3.at[kind, which, q], r3.at[kind, q], order.at(a, b, to)).start()

                @pl.when(jnp.logical_not(away))
                def _():
                    for low in range(2):
                        src, dst = piece(kind, which, q, low)
                        pltpu.make_async_copy(src, dst, c3.at[kind, q]).start()

            pass_on(0)

            @pl.when(order.has_second(a, b))
            def _():
                pass_on(1)

    eye = lax.broadcasted_iota(jnp.int32, (256, 256), 0) == lax.broadcasted_iota(jnp.int32, (256, 256), 1)

    def block(which, q, part):
        return rows[which, q, part].reshape(256, 1024)

    def chunk(which, q):
        return rows[which, q].reshape(512, 1024)

    def scores(left, right):
        return lax.dot_general(left, right, (((1,), (1,)), ((), ())), preferred_element_type=jnp.float32)

    def by_column(which, q, part, level, cols, power):
        shaped = level.shape[0] // 8, 8, 128
        high[which, q, part, :, cols] = jnp.maximum(high[which, q, part, :, cols], jnp.max(level.reshape(shaped), axis=0))
        total[which, q, part, :, cols] = total[which, q, part, :, cols] + jnp.sum(power.reshape(shaped), axis=0)

    def both_ways(left, right, own_q, lines, which, q, part):
        score = scores(left, right)
        row_veil = shade[own_q, lines]
        levels, powers = [], []
        for lane in range(2):
            cols = slice(lane * 128, lane * 128 + 128)
            level = score[:, cols] * SHARP + (row_veil + veil[which, q, part, 0:1, cols])
            power = jnp.exp2(level)
            by_column(which, q, part, level, cols, power)
            levels.append(level)
            powers.append(power)
        side_high[own_q, lines] = jnp.maximum(side_high[own_q, lines], jnp.maximum(levels[0], levels[1]))
        side_total[own_q, lines] = side_total[own_q, lines] + (powers[0] + powers[1])

    def own_pairs(q):
        me = chunk(0, q)
        score = [scores(me, block(0, q, part)) for part in range(2)]
        for part in range(2):
            square = jnp.where(eye, score[part][part * 256 : part * 256 + 256], 0.0)
            there = jnp.where(jnp.sum(square, axis=1, keepdims=True) > 0.5, 0.0, ABSENT)
            shade[q, part * 256 : part * 256 + 256] = jnp.broadcast_to(there, (256, 128))
            seen = jnp.sum(square, axis=0, keepdims=True) > 0.5
            veil[0, q, part] = jnp.broadcast_to(jnp.where(seen, -SHARP, ABSENT), (8, 256))
        for part in range(2):
            for lane in range(2):
                cols = slice(lane * 128, lane * 128 + 128)
                level = score[part][:, cols] * SHARP + (shade[q] - SHARP)
                here = level[part * 256 : part * 256 + 256]
                here = jnp.where(eye[:, cols], ABSENT, here)
                rest = level[256 - part * 256 : 512 - part * 256]
                by_column(0, q, part, here, cols, jnp.exp2(here))
                by_column(0, q, part, rest, cols, jnp.exp2(rest))
        if q:
            @pl.loop(0, q)
            def _(old):
                left = chunk(0, old)
                for part in range(2):
                    both_ways(left, block(0, q, part), old, slice(0, 512), 0, q, part)

    def cross_pairs(q):
        for part in range(2):
            right = block(1, q, part)
            square = jnp.where(eye, scores(right, right), 0.0)
            seen = jnp.sum(square, axis=0, keepdims=True) > 0.5
            veil[1, q, part] = jnp.broadcast_to(jnp.where(seen, -SHARP, ABSENT), (8, 256))
        for mine in range(2):
            part = lax.rem(mine + core, 2)
            both_ways(
                block(0, q, mine), block(1, q, part), q, slice(mine * 256, mine * 256 + 256), 1, q, part
            )
        if q:
            @pl.loop(0, q)
            def _(old):
                left = chunk(0, old)
                for part in range(2):
                    both_ways(left, block(1, q, part), old, slice(0, 512), 1, q, part)

    def arrive(q):
        for kind in range(3):
            drain(pk[kind].at[0], r3.at[kind, q])
            drain(rb[kind].at[0, 0, 0], c3.at[kind, q])
        remote(rows.at[0, q], rows.at[1, q], sx.at[q], rx.at[q], peer).start()

    def process(q):
        arrive(q)
        own_pairs(q)
        drain(rows.at[1, q], rx.at[q])
        cross_pairs(q)

    second_phase(0)
    for q in range(4):
        third_phase(q)
        if q == 0:
            second_phase(1)
        if q:
            @pl.when(is_root)
            def _():
                process(q - 1)

    @pl.when(is_root)
    def _():
        process(3)
        for q in range(4):
            for part in range(2):
                spot = 2 * q + part
                swap[0, spot : spot + 1] = jnp.max(high[1, q, part], axis=0, keepdims=True)
                swap[1, spot : spot + 1] = jnp.sum(total[1, q, part], axis=0, keepdims=True)
        remote(swap, swapped, se, re, peer).start()
        tops, masses = [], []
        for q in range(4):
            for part in range(2):
                lines = slice(part * 256, part * 256 + 256)
                side = jnp.max(side_high[q, lines].T.reshape(16, 8, 256), axis=0)
                tops.append(jnp.max(jnp.maximum(high[0, q, part], side), axis=0, keepdims=True))
                side = jnp.sum(side_total[q, lines].T.reshape(16, 8, 256), axis=0)
                masses.append(jnp.sum(total[0, q, part] + side, axis=0, keepdims=True))
        drain(swapped, re)
        for q in range(4):
            for part in range(2):
                spot = 2 * q + part
                present = veil[0, q, part, 0:1] > 0.5 * ABSENT
                top = jnp.maximum(tops[spot], swapped[0, spot : spot + 1])
                mass = masses[spot] + swapped[1, spot : spot + 1]
                paired = present & (top > 0.5 * ABSENT)
                near = jnp.where(paired, top * (1.0 / SHARP) + 1.0, -2.0)
                stats[part, q : q + 1] = jnp.where(present, near, 0.0)
                stats[part, 4 + q : 5 + q] = jnp.where(paired, 20.0 + jnp.log(jnp.where(paired, mass, 1.0)), 0.0)
        spot = root_l * 2 + core
        for row in range(4):
            for column in range(4):
                target = device(column, y, row, lax.rem(root_g, 2))
                same = (x == column) & (z == row) & (core == lax.rem(root_g, 2))

                @pl.when(jnp.logical_not(same))
                def _():
                    remote(stats.at[row % 2], landed.at[spot], so, ro, target).start()

                @pl.when(same)
                def _():
                    copy = pltpu.make_async_copy(stats.at[row % 2], landed.at[spot], co)
                    copy.start()
                    copy.wait()

    in_mine = jnp.int32(0)
    for l in range(3):
        qx, qy, qz = root_of(g, l)
        in_mine = in_mine + jnp.where((qx == x) & (qy == y) & (qz == z), 1, 0)

    @pl.when(in_mine == 0)
    def _():
        drain(landed, ro)

    @pl.when(in_mine != 0)
    def _():
        drain(landed.at[pl.ds(0, 5)], ro)

    lane = lax.broadcasted_iota(jnp.int32, (48, 256), 1)
    held = landed[...].reshape(48, 256)
    moved = []
    for odd in range(2):
        yl = lax.rem(odd + z + x, 2)
        kept = jnp.zeros((48, 256), jnp.float32)
        for yh in range(2):
            start = yl * 128 + (z // 2) * 64 + yh * 32 + (x // 2) * 16
            end = yh * 128 + yl * 64
            turned = pltpu.roll(held, lax.rem(end - start + 256, 256), 1)
            kept = kept + jnp.where((lane >= end) & (lane < end + 16), turned, 0.0)
        moved.append(kept)
    near = [jnp.zeros((1, 256), jnp.float32)] * 3
    lse = [jnp.zeros((1, 256), jnp.float32)] * 3
    for k in range(2):
        for half in range(HALVES):
            shift = k * 32 + half * 16
            for odd in range(2):
                turned = pltpu.roll(moved[odd], shift, 1) if shift else moved[odd]
                for l in range(3):
                    line = (2 * l + k) * 8 + half * 2 + odd
                    near[l] = near[l] + turned[line : line + 1]
                    lse[l] = lse[l] + turned[line + 4 : line + 5]
    for l in range(3):
        near_out[0, 0, l : l + 1] = near[l]
        lse_out[0, 0, l : l + 1] = lse[l]

    for half in range(HALVES):
        for kind, order in enumerate(orders):
            a, b, c = order.a, order.b, order.c
            drain(pk[kind].at[half, pl.ds(0, 3)], s1.at[kind, half])
            drain(pk[kind].at[half, pl.ds(0, 2)], s2.at[kind, half, 0])
            for step in (1, 2, 3):
                @pl.when(order.has_second(a, mod4(b + step)))
                def _():
                    drain(rb[kind].at[0, 0, 0, 0], s2.at[kind, half, 1])

    for kind, order in enumerate(orders):
        for which in range(2):
            away, _ = sends(kind, which)
            if which:
                away = away & order.has_second(order.a, order.b)

            @pl.when(away)
            def _():
                drain(rb[kind].at[0, 0, 0], s3.at[kind, which, 3])

                @pl.when(is_root)
                def _():
                    for q in range(3):
                        drain(rb[kind].at[0, 0, 0], s3.at[kind, which, q])

    @pl.when(is_root)
    def _():
        for q in range(4):
            drain(rows.at[0, q], sx.at[q])
        drain(swap, se)
        for count in range(15):
            drain(stats.at[0], so)

        @pl.when(core != lax.rem(root_g, 2))
        def _():
            drain(stats.at[0], so)


def solution(mesh):
    def step(embeds, cluster_id, owner_slot):
        n, width = embeds.shape
        bf, f32 = jnp.bfloat16, jnp.float32
        widths = [hi - lo for lo, hi in COLS]
        vmem = pltpu.VMEM
        dma = pltpu.SemaphoreType.DMA
        return pl.pallas_call(
            kernel,
            out_shape=[jax.ShapeDtypeStruct((1, 1, 3, 256), f32)] * 2,
            in_specs=[
                pl.BlockSpec(memory_space=pl.ANY),
                pl.BlockSpec(memory_space=pltpu.VMEM),
                pl.BlockSpec(memory_space=pltpu.SMEM),
            ],
            out_specs=[pl.BlockSpec(memory_space=pltpu.VMEM)] * 2,
            scratch_shapes=[vmem((n, width), bf), vmem((n, width), bf)]
            + [vmem((2, 4, 6, 16, w), bf) for w in widths]
            + [vmem((2, 2, 2, 6, 16, w), bf) for w in widths]
            + [vmem((2, 2, 2, 2, 2, 2, 16, w), bf) for w in widths]
            + [
                vmem((2, 4, 2, 2, 2, 2, 2, 16, width), bf),
                vmem((4, 512, 128), f32),
                vmem((2, 4, 2, 8, 256), f32),
                vmem((2, 4, 2, 8, 256), f32),
                vmem((2, 4, 2, 8, 256), f32),
                vmem((4, 512, 128), f32),
                vmem((4, 512, 128), f32),
                vmem((2, 8, 256), f32),
                vmem((2, 8, 256), f32),
                vmem((2, 8, 256), f32),
                vmem((6, 8, 256), f32),
                dma, dma((3, 2)), dma((3, 2)), dma((3, 2)),
                dma((3, 2, 2)), dma((3, 2, 2)), dma((3, 2, 2)),
                dma((3, 2, 4)), dma((3, 4)), dma((3, 4)),
                dma((4,)), dma((4,)), dma, dma, dma, dma, dma,
            ],
            compiler_params=pltpu.CompilerParams(
                collective_id=0, has_side_effects=True, vmem_limit_bytes=56 * 1024 * 1024
            ),
        )(embeds, cluster_id, owner_slot)

    return jax.shard_map(
        step,
        mesh=mesh,
        in_specs=(P(("group", "dev"), None), P(("group", "dev")), P()),
        out_specs=(P("group", "dev", None, None), P("group", "dev", None, None)),
        check_vma=False,
    )
```

```python
import functools
import math

import jax
import jax.numpy as jnp
from jax import lax
from jax.experimental import pallas as pl
from jax.experimental.pallas import tpu as pltpu
from jax.sharding import PartitionSpec as P

MESH = pl.DeviceIdType.MESH
SHARP = 20.0 * math.log2(math.e)
ABSENT = -1e30
COLS = ((0, 384), (384, 768), (768, 1024))
HALVES = 2


def mod4(value):
    return lax.rem(value + 16, 4)


def place():
    g = lax.axis_index("group")
    d = lax.axis_index("dev")
    return mod4(lax.rem(d, 4) + 0), mod4(g // 2 + 0), mod4(d // 4 + 1), lax.rem(g, 2)


def device(x, y, z, core):
    return (mod4(y - 0) * 2 + core, mod4(z - 1) * 4 + mod4(x - 0))


def root_of(g, l):
    y = g // 2
    if l < 2:
        x = lax.rem(g, 2) * 2 + l
        return x, y, mod4(x + y)
    x = mod4(y - lax.rem(g, 2))
    return x, y, mod4(x + y + 2)


def slot_positions(own):
    g = (own * 11) >> 5
    l = own - 3 * g
    y = g >> 1
    odd = g & 1
    second = l == 2
    x = jnp.where(second, (y - odd) & 3, odd * 2 + l)
    z = jnp.where(second, x + y + 2, x + y) & 3
    return (
        x * 6 + jnp.where(second, 4 + odd, y),
        y * 6 + jnp.where(second, 5 - odd, z),
        z * 6 + jnp.where(second, 4 + (x >> 1), x),
    )


class Order:
    def __init__(self, kind, x, y, z, core):
        self.kind = kind
        self.a, self.b, self.c = ((x, y, z), (y, z, x), (z, x, y))[kind]
        self.core = core

    def at(self, a, b, c):
        x, y, z = ((a, b, c), (c, a, b), (b, c, a))[self.kind]
        return device(x, y, z, self.core)

    def first(self, a, b):
        return mod4((a + b, b - a, a - b)[self.kind])

    def has_second(self, a, b):
        if self.kind == 0:
            return mod4(b - a) < 2
        if self.kind == 1:
            return mod4(b - 2 * a - 1) < 2
        return (a < 2) == (lax.rem(b, 2) == 1)

    def second_slot(self, a, b):
        return 4 + (mod4(b - a), mod4(b - 2 * a - 1), b // 2)[self.kind]


def kernel(
    embeds, cluster_id, owner_slot, both_out,
    raw, cid, owner, unit, pk0, pk1, pk2, ra0, ra1, ra2, rb0, rb1, rb2, rows, shade, veil, high, total, side_high, side_total, stats, landed,
    in_sem, id_sem, owner_sem, s1, r1, c1, s2, r2, c2, s3, r3, c3, sx, rx, sv, rv, so, ro, co,
):
    x, y, z, core = place()
    pk, ra, rb = (pk0, pk1, pk2), (ra0, ra1, ra2), (rb0, rb1, rb2)
    orders = [Order(kind, x, y, z, core) for kind in range(3)]
    is_first = z == mod4(x + y)
    is_second = (z == mod4(x + y + 2)) & (mod4(y - x) < 2)
    is_root = is_first | is_second
    root_g = jnp.where(is_first, 2 * y + x // 2, 2 * y + mod4(y - x))
    root_l = jnp.where(is_first, lax.rem(x, 2), 2)
    peer = device(x, y, z, 1 - core)
    g = lax.axis_index("group")

    barrier = pltpu.get_barrier_semaphore()

    def greet(target):
        pl.semaphore_signal(barrier, inc=1, device_id=target, device_id_type=MESH)

    for step in (1, 2, 3):
        greet(device(mod4(x + step), y, z, core))
        greet(device(x, mod4(y + step), z, core))
        greet(device(x, y, mod4(z + step), core))
    greet(peer)
    fetch = pltpu.make_async_copy(embeds, raw, in_sem)
    fetch_ids = pltpu.make_async_copy(cluster_id, cid, id_sem)
    fetch_owner = pltpu.make_async_copy(owner_slot, owner, owner_sem)
    fetch_ids.start()
    fetch_owner.start()
    fetch.start()

    n = raw.shape[0]
    fetch_ids.wait()
    fetch_owner.wait()
    ids = cid[...].reshape(1, n)
    own = jnp.zeros_like(ids)
    for c in range(24):
        own = jnp.where(ids == c, owner[c], own)
    member = (lax.broadcasted_iota(jnp.int32, (32, n), 0) == ids).astype(jnp.float32)
    earlier = lax.broadcasted_iota(jnp.int32, (n, n), 0) < lax.broadcasted_iota(jnp.int32, (n, n), 1)
    before = jnp.dot(
        member.astype(jnp.bfloat16), earlier.astype(jnp.float32).astype(jnp.bfloat16), preferred_element_type=jnp.float32
    )
    rank = jnp.sum(member * before, axis=0, keepdims=True).astype(jnp.int32)
    spots = [slot * 16 + (rank & 15) + (rank >> 4) * 384 for slot in slot_positions(own)]

    fetch.wait()
    wide = raw[...].astype(jnp.float32)
    scale = lax.rsqrt(jnp.sum(wide * wide, axis=1, keepdims=True) + 1e-6)
    unit[...] = (wide * scale).astype(jnp.bfloat16)

    targets = lax.broadcasted_iota(jnp.int32, (384, n), 0)
    for half in range(HALVES):
        for kind, (lo, hi) in enumerate(COLS):
            pick = (targets == spots[kind] - half * 384).astype(jnp.float32).astype(jnp.bfloat16)
            moved = jnp.dot(pick, unit[:, lo:hi], preferred_element_type=jnp.float32)
            pk[kind][half] = moved.astype(jnp.bfloat16).reshape(4, 6, 16, hi - lo)

    @pl.when(is_root)
    def _():
        high[...] = jnp.full(high.shape, ABSENT, jnp.float32)
        total[...] = jnp.zeros(total.shape, jnp.float32)
        side_high[...] = jnp.full(side_high.shape, ABSENT, jnp.float32)
        side_total[...] = jnp.zeros(side_total.shape, jnp.float32)

    pl.semaphore_wait(barrier, 10)

    def remote(src, dst, send, recv, target):
        return pltpu.make_async_remote_copy(
            src_ref=src, dst_ref=dst, send_sem=send, recv_sem=recv, device_id=target, device_id_type=MESH
        )

    def drain(ref, sem):
        pltpu.make_async_copy(ref, ref, sem).wait()

    def first_phase(half):
        for kind, order in enumerate(orders):
            a, b, c = order.a, order.b, order.c
            for step in (1, 2, 3):
                to = mod4(a + step)
                remote(
                    pk[kind].at[half, to], ra[kind].at[half, a // 2, lax.rem(a, 2)],
                    s1.at[kind, half], r1.at[kind, half], order.at(to, b, c),
                ).start()
            pltpu.make_async_copy(
                pk[kind].at[half, a], ra[kind].at[half, a // 2, lax.rem(a, 2)], c1.at[kind, half]
            ).start()

    def landing(kind, which, half, b):
        if kind == 2:
            return rb[kind].at[which, half, :, :, b // 2, lax.rem(b, 2)]
        return rb[kind].at[which, half, b // 2, lax.rem(b, 2)]

    def second_phase(half):
        for kind, order in enumerate(orders):
            a, b, c = order.a, order.b, order.c
            drain(pk[kind].at[half, pl.ds(0, 3)], r1.at[kind, half])
            drain(pk[kind].at[half, 0], c1.at[kind, half])
            for step in (1, 2, 3):
                to = mod4(b + step)
                remote(
                    ra[kind].at[half, :, :, to], landing(kind, 0, half, b),
                    s2.at[kind, half, 0], r2.at[kind, half, 0], order.at(a, to, c),
                ).start()

                @pl.when(order.has_second(a, to))
                def _():
                    remote(
                        ra[kind].at[half, :, :, order.second_slot(a, to)], landing(kind, 1, half, b),
                        s2.at[kind, half, 1], r2.at[kind, half, 1], order.at(a, to, c),
                    ).start()

            pltpu.make_async_copy(ra[kind].at[half, :, :, b], landing(kind, 0, half, b), c2.at[kind, half, 0]).start()

            @pl.when(order.has_second(a, b))
            def _():
                pltpu.make_async_copy(
                    ra[kind].at[half, :, :, order.second_slot(a, b)], landing(kind, 1, half, b), c2.at[kind, half, 1]
                ).start()

    def piece(kind, which, q, low):
        lo, hi = COLS[kind]
        half, odd = q // 2, q % 2
        cols = pl.ds(lo, hi - lo)
        xl, yl, zl = lax.rem(x, 2), lax.rem(y, 2), lax.rem(z, 2)
        if kind == 0:
            other = lax.rem(odd + zl + low, 2)
            dst = rows.at[0, q, zl, z // 2, low, :, :, :, cols]
        elif kind == 1:
            other = lax.rem(odd + xl + low, 2)
            dst = rows.at[0, q, low, :, other, :, x // 2, :, cols]
        else:
            other = lax.rem(odd + yl + low, 2)
            dst = rows.at[0, q, low, :, yl, y // 2, :, :, cols]
        return rb[kind].at[which, half, :, low, :, other], dst

    def sends(kind, which):
        order = orders[kind]
        to = mod4(order.first(order.a, order.b) + 2 * which)
        return order.c != to, to

    def third_phase(q):
        half = q // 2
        for kind, order in enumerate(orders):
            a, b = order.a, order.b

            def pass_on(which):
                if q % 2 == 0:
                    drain(pk[kind].at[half, pl.ds(0, 2)], r2.at[kind, half, which])
                    drain(rb[kind].at[0, 0, 0, 0], c2.at[kind, half, which])
                away, to = sends(kind, which)

                @pl.when(away)
                def _():
                    for low in range(2):
                        if q:
                            @pl.when(jnp.logical_not(is_root))
                            def _():
                                drain(rb[kind].at[0, 0, 0, 0], s3.at[kind, which, q - 1, low])

                        src, dst = piece(kind, which, q, low)
                        remote(src, dst, s3.at[kind, which, q, low], r3.at[kind, q], order.at(a, b, to)).start()

                @pl.when(jnp.logical_not(away))
                def _():
                    for low in range(2):
                        src, dst = piece(kind, which, q, low)
                        pltpu.make_async_copy(src, dst, c3.at[kind, q]).start()

            pass_on(0)

            @pl.when(order.has_second(a, b))
            def _():
                pass_on(1)

    eye = lax.broadcasted_iota(jnp.int32, (256, 256), 0) == lax.broadcasted_iota(jnp.int32, (256, 256), 1)

    def block(which, q, part):
        return rows[which, q, part].reshape(256, 1024)

    def chunk(which, q):
        return rows[which, q].reshape(512, 1024)

    def scores(left, right):
        return lax.dot_general(left, right, (((1,), (1,)), ((), ())), preferred_element_type=jnp.float32)

    strip = 64

    def fold(values, merge):
        return merge(values.reshape(values.shape[0] // 8, 8, 128), axis=0)

    def merge_columns(which, q, part, tops, masses):
        for lane in range(2):
            cols = slice(lane * 128, lane * 128 + 128)
            high[which, q, part, :, cols] = jnp.maximum(high[which, q, part, :, cols], tops[lane])
            total[which, q, part, :, cols] = total[which, q, part, :, cols] + masses[lane]

    def both_ways(left, right, own_q, first, which, q, part):
        score = scores(left, right)
        tops, masses = [None, None], [None, None]
        for row in range(0, left.shape[0], strip):
            lines = slice(first + row, first + row + strip)
            row_veil = shade[own_q, lines]
            levels, powers = [], []
            for lane in range(2):
                cols = slice(lane * 128, lane * 128 + 128)
                level = score[row : row + strip, cols] * SHARP + (row_veil + veil[which, q, part, 0:1, cols])
                power = jnp.exp2(level)
                top, mass = fold(level, jnp.max), fold(power, jnp.sum)
                tops[lane] = top if row == 0 else jnp.maximum(tops[lane], top)
                masses[lane] = mass if row == 0 else masses[lane] + mass
                levels.append(level)
                powers.append(power)
            side_high[own_q, lines] = jnp.maximum(side_high[own_q, lines], jnp.maximum(levels[0], levels[1]))
            side_total[own_q, lines] = side_total[own_q, lines] + (powers[0] + powers[1])
        merge_columns(which, q, part, tops, masses)

    def own_pairs(q):
        me = chunk(0, q)
        score = [scores(me, block(0, q, part)) for part in range(2)]
        for part in range(2):
            square = jnp.where(eye, score[part][part * 256 : part * 256 + 256], 0.0)
            there = jnp.where(jnp.sum(square, axis=1, keepdims=True) > 0.5, 0.0, ABSENT)
            shade[q, part * 256 : part * 256 + 256] = jnp.broadcast_to(there, (256, 128))
            seen = jnp.sum(square, axis=0, keepdims=True) > 0.5
            veil[0, q, part] = jnp.broadcast_to(jnp.where(seen, -SHARP, ABSENT), (8, 256))
        remote(veil.at[0, q], veil.at[1, q], sv.at[q], rv.at[q], peer).start()
        for part in range(2):
            tops, masses = [None, None], [None, None]
            for row in range(0, 512, strip):
                for lane in range(2):
                    cols = slice(lane * 128, lane * 128 + 128)
                    level = score[part][row : row + strip, cols] * SHARP + (shade[q, row : row + strip] - SHARP)
                    if row // 256 == part:
                        level = jnp.where(eye[row % 256 : row % 256 + strip, cols], ABSENT, level)
                    top, mass = fold(level, jnp.max), fold(jnp.exp2(level), jnp.sum)
                    tops[lane] = top if row == 0 else jnp.maximum(tops[lane], top)
                    masses[lane] = mass if row == 0 else masses[lane] + mass
            merge_columns(0, q, part, tops, masses)
        for old in range(q):
            left = chunk(0, old)
            for part in range(2):
                both_ways(left, block(0, q, part), old, 0, 0, q, part)

    def cross_pairs(q):
        for mine in range(2):
            part = lax.rem(mine + core, 2)
            both_ways(
                block(0, q, mine), block(1, q, part), q, mine * 256, 1, q, part
            )
        for old in range(q):
            left = chunk(0, old)
            for part in range(2):
                both_ways(left, block(1, q, part), old, 0, 1, q, part)

    def arrive(q):
        for kind in range(3):
            drain(pk[kind].at[0], r3.at[kind, q])
            drain(rb[kind].at[0, 0, 0], c3.at[kind, q])
            lo, hi = COLS[kind]
            cols = pl.ds(lo, hi - lo)
            remote(
                rows.at[0, q, :, :, :, :, :, :, cols], rows.at[1, q, :, :, :, :, :, :, cols],
                sx.at[kind, q], rx.at[kind, q], peer,
            ).start()

    def process(q):
        if q not in (2, 3):
            arrive(q)
        own_pairs(q)
        for kind in range(3):
            drain(rb[kind].at[0], rx.at[kind, q])
        drain(veil.at[1, q], rv.at[q])
        if q + 1 in (2, 3):
            arrive(q + 1)
        cross_pairs(q)

    first_phase(0)
    first_phase(1)
    second_phase(0)
    second_phase(1)
    third_phase(0)
    third_phase(1)
    third_phase(2)
    third_phase(3)

    @pl.when(is_root)
    def _():
        process(0)


    @pl.when(is_root)
    def _():
        process(1)


    @pl.when(is_root)
    def _():
        process(2)


    @pl.when(is_root)
    def _():
        process(3)
        for q in range(4):
            for part in range(2):
                lines = slice(part * 256, part * 256 + 256)
                side = jnp.max(side_high[q, lines].T.reshape(16, 8, 256), axis=0)
                top = jnp.max(jnp.maximum(high[0, q, part], side), axis=0, keepdims=True)
                top = jnp.where(veil[0, q, part, 0:1] > 0.5 * ABSENT, top, -ABSENT)
                side = jnp.sum(side_total[q, lines].T.reshape(16, 8, 256), axis=0)
                mass = jnp.sum(total[0, q, part] + side, axis=0, keepdims=True)
                far_top = jnp.max(high[1, q, part], axis=0, keepdims=True)
                far_mass = jnp.sum(total[1, q, part], axis=0, keepdims=True)
                for line, value in ((q, top), (4 + q, mass), (8 + q, far_top), (12 + q, far_mass)):
                    for lane in range(2):
                        stats[part, lane, line : line + 1] = value[:, lane * 128 : lane * 128 + 128]
        spot = root_l * 2 + core
        for step in range(16):
            row = mod4(z + step // 4)
            column = mod4(x + step % 4)
            target = device(column, y, row, lax.rem(root_g, 2))
            src = stats.at[lax.rem(row, 2), row // 2]
            if step:
                remote(src, landed.at[spot], so, ro, target).start()
            else:
                same = core == lax.rem(root_g, 2)

                @pl.when(jnp.logical_not(same))
                def _():
                    remote(src, landed.at[spot], so, ro, target).start()

                @pl.when(same)
                def _():
                    copy = pltpu.make_async_copy(src, landed.at[spot], co)
                    copy.start()
                    copy.wait()

    for half in range(HALVES):
        for kind, order in enumerate(orders):
            a, b, c = order.a, order.b, order.c
            drain(pk[kind].at[half, pl.ds(0, 3)], s1.at[kind, half])
            drain(pk[kind].at[half, pl.ds(0, 2)], s2.at[kind, half, 0])
            for step in (1, 2, 3):
                @pl.when(order.has_second(a, mod4(b + step)))
                def _():
                    drain(rb[kind].at[0, 0, 0, 0], s2.at[kind, half, 1])

    for kind, order in enumerate(orders):
        for which in range(2):
            away, _ = sends(kind, which)
            if which:
                away = away & order.has_second(order.a, order.b)

            @pl.when(away)
            def _():
                for low in range(2):
                    drain(rb[kind].at[0, 0, 0, 0], s3.at[kind, which, 3, low])

                @pl.when(is_root)
                def _():
                    for q in range(3):
                        for low in range(2):
                            drain(rb[kind].at[0, 0, 0, 0], s3.at[kind, which, q, low])

    @pl.when(is_root)
    def _():
        for q in range(4):
            for kind in range(3):
                drain(rb[kind].at[0], sx.at[kind, q])
            drain(veil.at[0, q], sv.at[q])
        for count in range(15):
            drain(stats.at[0, 0], so)

        @pl.when(core != lax.rem(root_g, 2))
        def _():
            drain(stats.at[0, 0], so)

    in_mine = jnp.int32(0)
    for l in range(3):
        qx, qy, qz = root_of(g, l)
        in_mine = in_mine + jnp.where((qx == x) & (qy == y) & (qz == z), 1, 0)

    @pl.when(in_mine == 0)
    def _():
        drain(landed, ro)

    @pl.when(in_mine != 0)
    def _():
        drain(landed.at[pl.ds(0, 5)], ro)

    lane = lax.broadcasted_iota(jnp.int32, (48, 128), 1)
    first = lax.broadcasted_iota(jnp.int32, (8, 128), 0) < 4
    final = []
    for l in range(3):
        for k in range(2):
            mine, other = landed[2 * l + k], landed[2 * l + 1 - k]
            top = jnp.maximum(mine[0:4], other[8:12])
            mass = mine[4:8] + other[12:16]
            top = jnp.concatenate([top, top], axis=0)
            mass = jnp.concatenate([mass, mass], axis=0)
            paired = top > 0.5 * ABSENT
            near_row = jnp.where(paired, top * (1.0 / SHARP) + 1.0, -2.0)
            lse_row = jnp.where(paired, 20.0 + jnp.log(jnp.where(paired, mass, 1.0)), 0.0)
            final.append(jnp.where(top > -0.5 * ABSENT, 0.0, jnp.where(first, near_row, lse_row)))
    held = jnp.concatenate(final, axis=0)
    out = [[jnp.zeros((1, 128), jnp.float32) for _ in range(6)] for _ in range(2)]
    for yh in range(2):
        turned = pltpu.roll(held, lax.rem(256 - yh * 32 - (x // 2) * 16, 128), 1)
        for odd in range(2):
            start = lax.rem(odd + z + x, 2) * 64
            kept = jnp.where((lane >= start) & (lane < start + 16), turned, 0.0)
            for k in range(2):
                for half in range(HALVES):
                    shift = k * 32 + half * 16
                    moved = pltpu.roll(kept, shift, 1) if shift else kept
                    for l in range(3):
                        line = (2 * l + k) * 8 + half * 2 + odd
                        out[yh][l] = out[yh][l] + moved[line : line + 1]
                        out[yh][3 + l] = out[yh][3 + l] + moved[line + 4 : line + 5]
        for which in range(2):
            for l in range(3):
                both_out[which, l, :, yh * 128 : yh * 128 + 128] = out[yh][3 * which + l]


def solution(mesh):
    def step(embeds, cluster_id, owner_slot):
        n, width = embeds.shape
        bf, f32 = jnp.bfloat16, jnp.float32
        widths = [hi - lo for lo, hi in COLS]
        vmem = pltpu.VMEM
        dma = pltpu.SemaphoreType.DMA
        both = pl.pallas_call(
            kernel,
            out_shape=jax.ShapeDtypeStruct((2, 3, 1, 256), f32),
            in_specs=[pl.BlockSpec(memory_space=pl.ANY)] * 3,
            out_specs=pl.BlockSpec(memory_space=pltpu.VMEM),
            scratch_shapes=[vmem((n, width), bf), vmem((n,), jnp.int32), pltpu.SMEM((24,), jnp.int32), vmem((n, width), bf)]
            + [vmem((2, 4, 6, 16, w), bf) for w in widths]
            + [vmem((2, 2, 2, 6, 16, w), bf) for w in widths]
            + [vmem((2, 2, 2, 2, 2, 2, 16, w), bf) for w in widths]
            + [
                vmem((2, 4, 2, 2, 2, 2, 2, 16, width), bf),
                vmem((4, 512, 128), f32),
                vmem((2, 4, 2, 8, 256), f32),
                vmem((2, 4, 2, 8, 256), f32),
                vmem((2, 4, 2, 8, 256), f32),
                vmem((4, 512, 128), f32),
                vmem((4, 512, 128), f32),
                vmem((2, 2, 16, 128), f32),
                vmem((6, 16, 128), f32),
                dma, dma, dma, dma((3, 2)), dma((3, 2)), dma((3, 2)),
                dma((3, 2, 2)), dma((3, 2, 2)), dma((3, 2, 2)),
                dma((3, 2, 4, 2)), dma((3, 4)), dma((3, 4)),
                dma((3, 4)), dma((3, 4)), dma((4,)), dma((4,)), dma, dma, dma,
            ],
            compiler_params=pltpu.CompilerParams(
                collective_id=0, has_side_effects=True, vmem_limit_bytes=56 * 1024 * 1024
            ),
        )(embeds, cluster_id, owner_slot)
        return both[0].reshape(1, 1, 3, 256), both[1].reshape(1, 1, 3, 256)

    return jax.shard_map(
        step,
        mesh=mesh,
        in_specs=(P(("group", "dev"), None), P(("group", "dev")), P()),
        out_specs=(P("group", "dev", None, None), P("group", "dev", None, None)),
        check_vma=False,
    )
```

```python
import functools
import math

import jax
import jax.numpy as jnp
from jax import lax
from jax.experimental import pallas as pl
from jax.experimental.pallas import tpu as pltpu
from jax.sharding import PartitionSpec as P

MESH = pl.DeviceIdType.MESH
SHARP = 20.0 * math.log2(math.e)
ABSENT = -1e30
COLS = ((0, 384), (384, 768), (768, 1024))
HALVES = 2


def mod4(value):
    return lax.rem(value + 16, 4)


def place():
    g = lax.axis_index("group")
    d = lax.axis_index("dev")
    return mod4(lax.rem(d, 4) + 0), mod4(g // 2 + 0), mod4(d // 4 + 1), lax.rem(g, 2)


def device(x, y, z, core):
    return (mod4(y - 0) * 2 + core, mod4(z - 1) * 4 + mod4(x - 0))


def root_of(g, l):
    y = g // 2
    if l < 2:
        x = lax.rem(g, 2) * 2 + l
        return x, y, mod4(x + y)
    x = mod4(y - lax.rem(g, 2))
    return x, y, mod4(x + y + 2)


def slot_positions(own):
    g = (own * 11) >> 5
    l = own - 3 * g
    y = g >> 1
    odd = g & 1
    second = l == 2
    x = jnp.where(second, (y - odd) & 3, odd * 2 + l)
    z = jnp.where(second, x + y + 2, x + y) & 3
    return (
        x * 6 + jnp.where(second, 4 + odd, y),
        y * 6 + jnp.where(second, 5 - odd, z),
        z * 6 + jnp.where(second, 4 + (x >> 1), x),
    )


class Order:
    def __init__(self, kind, x, y, z, core):
        self.kind = kind
        self.a, self.b, self.c = ((x, y, z), (y, z, x), (z, x, y))[kind]
        self.core = core

    def at(self, a, b, c):
        x, y, z = ((a, b, c), (c, a, b), (b, c, a))[self.kind]
        return device(x, y, z, self.core)

    def first(self, a, b):
        return mod4((a + b, b - a, a - b)[self.kind])

    def has_second(self, a, b):
        if self.kind == 0:
            return mod4(b - a) < 2
        if self.kind == 1:
            return mod4(b - 2 * a - 1) < 2
        return (a < 2) == (lax.rem(b, 2) == 1)

    def second_slot(self, a, b):
        return 4 + (mod4(b - a), mod4(b - 2 * a - 1), b // 2)[self.kind]


def kernel(
    embeds, cluster_id, owner_slot, both_out,
    raw, cid, owner, unit, pk0, pk1, pk2, ra0, ra1, ra2, rb0, rb1, rb2, rl0, rl1, rl2, rows, shade, veil, high, total, side_high, side_total, stats, landed,
    in_sem, id_sem, owner_sem, s1, r1, c1, s2, r2, c2, s3, r3, c3, s4, r4, sx, rx, sv, rv, so, ro, co,
):
    x, y, z, core = place()
    pk, ra, rb, rl = (pk0, pk1, pk2), (ra0, ra1, ra2), (rb0, rb1, rb2), (rl0, rl1, rl2)
    orders = [Order(kind, x, y, z, core) for kind in range(3)]
    is_first = z == mod4(x + y)
    is_second = (z == mod4(x + y + 2)) & (mod4(y - x) < 2)
    is_root = is_first | is_second
    root_g = jnp.where(is_first, 2 * y + x // 2, 2 * y + mod4(y - x))
    root_l = jnp.where(is_first, lax.rem(x, 2), 2)
    peer = device(x, y, z, 1 - core)
    g = lax.axis_index("group")

    barrier = pltpu.get_barrier_semaphore()

    def greet(target):
        pl.semaphore_signal(barrier, inc=1, device_id=target, device_id_type=MESH)

    for step in (1, 2, 3):
        greet(device(mod4(x + step), y, z, core))
        greet(device(x, mod4(y + step), z, core))
        greet(device(x, y, mod4(z + step), core))
    greet(peer)
    fetch = pltpu.make_async_copy(embeds, raw, in_sem)
    fetch_ids = pltpu.make_async_copy(cluster_id, cid, id_sem)
    fetch_owner = pltpu.make_async_copy(owner_slot, owner, owner_sem)
    fetch_ids.start()
    fetch_owner.start()
    fetch.start()

    n = raw.shape[0]
    fetch_ids.wait()
    fetch_owner.wait()
    ids = cid[...].reshape(1, n)
    own = jnp.zeros_like(ids)
    for c in range(24):
        own = jnp.where(ids == c, owner[c], own)
    member = (lax.broadcasted_iota(jnp.int32, (32, n), 0) == ids).astype(jnp.float32)
    earlier = lax.broadcasted_iota(jnp.int32, (n, n), 0) < lax.broadcasted_iota(jnp.int32, (n, n), 1)
    before = jnp.dot(
        member.astype(jnp.bfloat16), earlier.astype(jnp.float32).astype(jnp.bfloat16), preferred_element_type=jnp.float32
    )
    rank = jnp.sum(member * before, axis=0, keepdims=True).astype(jnp.int32)
    spots = [slot * 16 + (rank & 15) + (rank >> 4) * 384 for slot in slot_positions(own)]

    fetch.wait()
    wide = raw[...].astype(jnp.float32)
    scale = lax.rsqrt(jnp.sum(wide * wide, axis=1, keepdims=True) + 1e-6)
    unit[...] = (wide * scale).astype(jnp.bfloat16)

    targets = lax.broadcasted_iota(jnp.int32, (384, n), 0)
    for half in range(HALVES):
        for kind, (lo, hi) in enumerate(COLS):
            pick = (targets == spots[kind] - half * 384).astype(jnp.float32).astype(jnp.bfloat16)
            moved = jnp.dot(pick, unit[:, lo:hi], preferred_element_type=jnp.float32)
            pk[kind][half] = moved.astype(jnp.bfloat16).reshape(4, 6, 16, hi - lo)

    @pl.when(is_root)
    def _():
        high[...] = jnp.full(high.shape, ABSENT, jnp.float32)
        total[...] = jnp.zeros(total.shape, jnp.float32)
        side_high[...] = jnp.full(side_high.shape, ABSENT, jnp.float32)
        side_total[...] = jnp.zeros(side_total.shape, jnp.float32)

    pl.semaphore_wait(barrier, 10)

    def remote(src, dst, send, recv, target):
        return pltpu.make_async_remote_copy(
            src_ref=src, dst_ref=dst, send_sem=send, recv_sem=recv, device_id=target, device_id_type=MESH
        )

    def drain(ref, sem):
        pltpu.make_async_copy(ref, ref, sem).wait()

    def first_phase(half):
        for kind, order in enumerate(orders):
            a, b, c = order.a, order.b, order.c
            for step in (1, 2, 3):
                to = mod4(a + step)
                remote(
                    pk[kind].at[half, to], ra[kind].at[half, a // 2, lax.rem(a, 2)],
                    s1.at[kind, half], r1.at[kind, half], order.at(to, b, c),
                ).start()
            pltpu.make_async_copy(
                pk[kind].at[half, a], ra[kind].at[half, a // 2, lax.rem(a, 2)], c1.at[kind, half]
            ).start()

    def landing(kind, which, half, b):
        if kind == 2:
            return rb[kind].at[which, half, :, :, b // 2, lax.rem(b, 2)]
        return rb[kind].at[which, half, b // 2, lax.rem(b, 2)]

    def second_phase(half):
        for kind, order in enumerate(orders):
            a, b, c = order.a, order.b, order.c
            drain(pk[kind].at[half, pl.ds(0, 3)], r1.at[kind, half])
            drain(pk[kind].at[half, 0], c1.at[kind, half])
            for step in (1, 2, 3):
                to = mod4(b + step)
                remote(
                    ra[kind].at[half, :, :, to], landing(kind, 0, half, b),
                    s2.at[kind, half, 0], r2.at[kind, half, 0], order.at(a, to, c),
                ).start()

                @pl.when(order.has_second(a, to))
                def _():
                    remote(
                        ra[kind].at[half, :, :, order.second_slot(a, to)], landing(kind, 1, half, b),
                        s2.at[kind, half, 1], r2.at[kind, half, 1], order.at(a, to, c),
                    ).start()

            pltpu.make_async_copy(ra[kind].at[half, :, :, b], landing(kind, 0, half, b), c2.at[kind, half, 0]).start()

            @pl.when(order.has_second(a, b))
            def _():
                pltpu.make_async_copy(
                    ra[kind].at[half, :, :, order.second_slot(a, b)], landing(kind, 1, half, b), c2.at[kind, half, 1]
                ).start()

    def piece(kind, which, q, low, c):
        lo, hi = COLS[kind]
        half, odd = q // 2, q % 2
        cols = pl.ds(lo, hi - lo)
        cl, ch = lax.rem(c, 2), c // 2
        other = lax.rem(odd + cl + low, 2)
        if kind == 0:
            dst = rows.at[0, q, cl, ch, low, :, :, :, cols]
        elif kind == 1:
            dst = rows.at[0, q, low, :, other, :, ch, :, cols]
        else:
            dst = rows.at[0, q, low, :, cl, ch, :, :, cols]
        return rb[kind].at[which, half, :, low, :, other], dst

    def sends(kind, which):
        order = orders[kind]
        to = mod4(order.first(order.a, order.b) + 2 * which)
        return order.c != to, to

    def third_phase(q):
        half = q // 2
        for kind, order in enumerate(orders):
            a, b = order.a, order.b

            def pass_on(which):
                if q % 2 == 0:
                    drain(pk[kind].at[half, pl.ds(0, 2)], r2.at[kind, half, which])
                    drain(rb[kind].at[0, 0, 0, 0], c2.at[kind, half, which])
                away, to = sends(kind, which)
                far = order.c == mod4(to + 2)

                def pace(low):
                    if q:
                        @pl.when(jnp.logical_not(is_root))
                        def _():
                            drain(rb[kind].at[0, 0, 0, 0], s3.at[kind, which, q - 1, low])

                @pl.when(away & jnp.logical_not(far))
                def _():
                    for low in range(2):
                        pace(low)
                        src, dst = piece(kind, which, q, low, order.c)
                        remote(src, dst, s3.at[kind, which, q, low], r3.at[kind, q], order.at(a, b, to)).start()

                @pl.when(far)
                def _():
                    for low in range(2):
                        pace(low)
                        src, _ = piece(kind, which, q, low, order.c)
                        remote(
                            src, rl[kind].at[which, q], s3.at[kind, which, q, low], r4.at[kind, which, q],
                            order.at(a, b, mod4(order.c + 1 + 2 * low)),
                        ).start()

                @pl.when(jnp.logical_not(away))
                def _():
                    for low in range(2):
                        src, dst = piece(kind, which, q, low, order.c)
                        pltpu.make_async_copy(src, dst, c3.at[kind, q]).start()

            pass_on(0)

            @pl.when(order.has_second(a, b))
            def _():
                pass_on(1)

    def beside(kind, which):
        away, to = sends(kind, which)
        near = away & (orders[kind].c != mod4(to + 2))
        if which:
            near = near & orders[kind].has_second(orders[kind].a, orders[kind].b)
        return near, to

    def relay(q):
        for kind, order in enumerate(orders):
            for which in range(2):
                near, to = beside(kind, which)

                @pl.when(near)
                def _():
                    drain(rb[kind].at[0, 0, 0, 0], r4.at[kind, which, q])
                    low = jnp.where(order.c == mod4(to + 3), 0, 1)
                    _, dst = piece(kind, which, q, low, mod4(to + 2))
                    remote(
                        rl[kind].at[which, q], dst, s4.at[kind, which, q], r3.at[kind, q], order.at(order.a, order.b, to)
                    ).start()

    eye = lax.broadcasted_iota(jnp.int32, (256, 256), 0) == lax.broadcasted_iota(jnp.int32, (256, 256), 1)

    def block(which, q, part):
        return rows[which, q, part].reshape(256, 1024)

    def chunk(which, q):
        return rows[which, q].reshape(512, 1024)

    def scores(left, right):
        return lax.dot_general(left, right, (((1,), (1,)), ((), ())), preferred_element_type=jnp.float32)

    strip = 64

    def fold(values, merge):
        return merge(values.reshape(values.shape[0] // 8, 8, 128), axis=0)

    def merge_columns(which, q, part, tops, masses):
        for lane in range(2):
            cols = slice(lane * 128, lane * 128 + 128)
            high[which, q, part, :, cols] = jnp.maximum(high[which, q, part, :, cols], tops[lane])
            total[which, q, part, :, cols] = total[which, q, part, :, cols] + masses[lane]

    def both_ways(left, right, own_q, first, which, q, part):
        score = scores(left, right)
        tops, masses = [None, None], [None, None]
        for row in range(0, left.shape[0], strip):
            lines = slice(first + row, first + row + strip)
            row_veil = shade[own_q, lines]
            levels, powers = [], []
            for lane in range(2):
                cols = slice(lane * 128, lane * 128 + 128)
                level = score[row : row + strip, cols] * SHARP + (row_veil + veil[which, q, part, 0:1, cols])
                power = jnp.exp2(level)
                top, mass = fold(level, jnp.max), fold(power, jnp.sum)
                tops[lane] = top if row == 0 else jnp.maximum(tops[lane], top)
                masses[lane] = mass if row == 0 else masses[lane] + mass
                levels.append(level)
                powers.append(power)
            side_high[own_q, lines] = jnp.maximum(side_high[own_q, lines], jnp.maximum(levels[0], levels[1]))
            side_total[own_q, lines] = side_total[own_q, lines] + (powers[0] + powers[1])
        merge_columns(which, q, part, tops, masses)

    def own_pairs(q):
        me = chunk(0, q)
        score = [scores(me, block(0, q, part)) for part in range(2)]
        for part in range(2):
            square = jnp.where(eye, score[part][part * 256 : part * 256 + 256], 0.0)
            there = jnp.where(jnp.sum(square, axis=1, keepdims=True) > 0.5, 0.0, ABSENT)
            shade[q, part * 256 : part * 256 + 256] = jnp.broadcast_to(there, (256, 128))
            seen = jnp.sum(square, axis=0, keepdims=True) > 0.5
            veil[0, q, part] = jnp.broadcast_to(jnp.where(seen, -SHARP, ABSENT), (8, 256))
        remote(veil.at[0, q], veil.at[1, q], sv.at[q], rv.at[q], peer).start()
        for part in range(2):
            tops, masses = [None, None], [None, None]
            for row in range(0, 512, strip):
                for lane in range(2):
                    cols = slice(lane * 128, lane * 128 + 128)
                    level = score[part][row : row + strip, cols] * SHARP + (shade[q, row : row + strip] - SHARP)
                    if row // 256 == part:
                        level = jnp.where(eye[row % 256 : row % 256 + strip, cols], ABSENT, level)
                    top, mass = fold(level, jnp.max), fold(jnp.exp2(level), jnp.sum)
                    tops[lane] = top if row == 0 else jnp.maximum(tops[lane], top)
                    masses[lane] = mass if row == 0 else masses[lane] + mass
            merge_columns(0, q, part, tops, masses)
        for old in range(q):
            left = chunk(0, old)
            for part in range(2):
                both_ways(left, block(0, q, part), old, 0, 0, q, part)

    def cross_pairs(q):
        for mine in range(2):
            part = lax.rem(mine + core, 2)
            both_ways(
                block(0, q, mine), block(1, q, part), q, mine * 256, 1, q, part
            )
        for old in range(q):
            left = chunk(0, old)
            for part in range(2):
                both_ways(left, block(1, q, part), old, 0, 1, q, part)

    def arrive(q):
        for kind in range(3):
            drain(pk[kind].at[0], r3.at[kind, q])
            drain(rb[kind].at[0, 0, 0], c3.at[kind, q])
            lo, hi = COLS[kind]
            cols = pl.ds(lo, hi - lo)
            remote(
                rows.at[0, q, :, :, :, :, :, :, cols], rows.at[1, q, :, :, :, :, :, :, cols],
                sx.at[kind, q], rx.at[kind, q], peer,
            ).start()

    def process(q):
        if q not in (2, 3):
            arrive(q)
        own_pairs(q)
        for kind in range(3):
            drain(rb[kind].at[0], rx.at[kind, q])
        drain(veil.at[1, q], rv.at[q])
        if q + 1 in (2, 3):
            arrive(q + 1)
        cross_pairs(q)

    first_phase(0)
    first_phase(1)
    second_phase(0)
    second_phase(1)
    third_phase(0)
    relay(0)
    third_phase(1)
    relay(1)
    third_phase(2)
    relay(2)
    third_phase(3)
    relay(3)

    @pl.when(is_root)
    def _():
        process(0)


    @pl.when(is_root)
    def _():
        process(1)


    @pl.when(is_root)
    def _():
        process(2)


    @pl.when(is_root)
    def _():
        process(3)
        for q in range(4):
            for part in range(2):
                lines = slice(part * 256, part * 256 + 256)
                side = jnp.max(side_high[q, lines].T.reshape(16, 8, 256), axis=0)
                top = jnp.max(jnp.maximum(high[0, q, part], side), axis=0, keepdims=True)
                top = jnp.where(veil[0, q, part, 0:1] > 0.5 * ABSENT, top, -ABSENT)
                side = jnp.sum(side_total[q, lines].T.reshape(16, 8, 256), axis=0)
                mass = jnp.sum(total[0, q, part] + side, axis=0, keepdims=True)
                far_top = jnp.max(high[1, q, part], axis=0, keepdims=True)
                far_mass = jnp.sum(total[1, q, part], axis=0, keepdims=True)
                for line, value in ((q, top), (4 + q, mass), (8 + q, far_top), (12 + q, far_mass)):
                    for lane in range(2):
                        stats[part, lane, line : line + 1] = value[:, lane * 128 : lane * 128 + 128]
        spot = root_l * 2 + core
        for step in range(16):
            row = mod4(z + step // 4)
            column = mod4(x + step % 4)
            target = device(column, y, row, lax.rem(root_g, 2))
            src = stats.at[lax.rem(row, 2), row // 2]
            if step:
                remote(src, landed.at[spot], so, ro, target).start()
            else:
                same = core == lax.rem(root_g, 2)

                @pl.when(jnp.logical_not(same))
                def _():
                    remote(src, landed.at[spot], so, ro, target).start()

                @pl.when(same)
                def _():
                    copy = pltpu.make_async_copy(src, landed.at[spot], co)
                    copy.start()
                    copy.wait()

    for half in range(HALVES):
        for kind, order in enumerate(orders):
            a, b, c = order.a, order.b, order.c
            drain(pk[kind].at[half, pl.ds(0, 3)], s1.at[kind, half])
            drain(pk[kind].at[half, pl.ds(0, 2)], s2.at[kind, half, 0])
            for step in (1, 2, 3):
                @pl.when(order.has_second(a, mod4(b + step)))
                def _():
                    drain(rb[kind].at[0, 0, 0, 0], s2.at[kind, half, 1])

    for kind in range(3):
        for which in range(2):
            near, _ = beside(kind, which)

            @pl.when(near)
            def _():
                for q in range(4):
                    drain(rb[kind].at[0, 0, 0, 0], s4.at[kind, which, q])

    for kind, order in enumerate(orders):
        for which in range(2):
            away, _ = sends(kind, which)
            if which:
                away = away & order.has_second(order.a, order.b)

            @pl.when(away)
            def _():
                for low in range(2):
                    drain(rb[kind].at[0, 0, 0, 0], s3.at[kind, which, 3, low])

                @pl.when(is_root)
                def _():
                    for q in range(3):
                        for low in range(2):
                            drain(rb[kind].at[0, 0, 0, 0], s3.at[kind, which, q, low])

    @pl.when(is_root)
    def _():
        for q in range(4):
            for kind in range(3):
                drain(rb[kind].at[0], sx.at[kind, q])
            drain(veil.at[0, q], sv.at[q])
        for count in range(15):
            drain(stats.at[0, 0], so)

        @pl.when(core != lax.rem(root_g, 2))
        def _():
            drain(stats.at[0, 0], so)

    in_mine = jnp.int32(0)
    for l in range(3):
        qx, qy, qz = root_of(g, l)
        in_mine = in_mine + jnp.where((qx == x) & (qy == y) & (qz == z), 1, 0)

    @pl.when(in_mine == 0)
    def _():
        drain(landed, ro)

    @pl.when(in_mine != 0)
    def _():
        drain(landed.at[pl.ds(0, 5)], ro)

    lane = lax.broadcasted_iota(jnp.int32, (48, 128), 1)
    first = lax.broadcasted_iota(jnp.int32, (8, 128), 0) < 4
    final = []
    for l in range(3):
        for k in range(2):
            mine, other = landed[2 * l + k], landed[2 * l + 1 - k]
            top = jnp.maximum(mine[0:4], other[8:12])
            mass = mine[4:8] + other[12:16]
            top = jnp.concatenate([top, top], axis=0)
            mass = jnp.concatenate([mass, mass], axis=0)
            paired = top > 0.5 * ABSENT
            near_row = jnp.where(paired, top * (1.0 / SHARP) + 1.0, -2.0)
            lse_row = jnp.where(paired, 20.0 + jnp.log(jnp.where(paired, mass, 1.0)), 0.0)
            final.append(jnp.where(top > -0.5 * ABSENT, 0.0, jnp.where(first, near_row, lse_row)))
    held = jnp.concatenate(final, axis=0)
    out = [[jnp.zeros((1, 128), jnp.float32) for _ in range(6)] for _ in range(2)]
    for yh in range(2):
        turned = pltpu.roll(held, lax.rem(256 - yh * 32 - (x // 2) * 16, 128), 1)
        for odd in range(2):
            start = lax.rem(odd + z + x, 2) * 64
            kept = jnp.where((lane >= start) & (lane < start + 16), turned, 0.0)
            for k in range(2):
                for half in range(HALVES):
                    shift = k * 32 + half * 16
                    moved = pltpu.roll(kept, shift, 1) if shift else kept
                    for l in range(3):
                        line = (2 * l + k) * 8 + half * 2 + odd
                        out[yh][l] = out[yh][l] + moved[line : line + 1]
                        out[yh][3 + l] = out[yh][3 + l] + moved[line + 4 : line + 5]
        for which in range(2):
            for l in range(3):
                both_out[which, l, :, yh * 128 : yh * 128 + 128] = out[yh][3 * which + l]


def solution(mesh):
    def step(embeds, cluster_id, owner_slot):
        n, width = embeds.shape
        bf, f32 = jnp.bfloat16, jnp.float32
        widths = [hi - lo for lo, hi in COLS]
        vmem = pltpu.VMEM
        dma = pltpu.SemaphoreType.DMA
        both = pl.pallas_call(
            kernel,
            out_shape=jax.ShapeDtypeStruct((2, 3, 1, 256), f32),
            in_specs=[pl.BlockSpec(memory_space=pl.ANY)] * 3,
            out_specs=pl.BlockSpec(memory_space=pltpu.VMEM),
            scratch_shapes=[vmem((n, width), bf), vmem((n,), jnp.int32), pltpu.SMEM((24,), jnp.int32), vmem((n, width), bf)]
            + [vmem((2, 4, 6, 16, w), bf) for w in widths]
            + [vmem((2, 2, 2, 6, 16, w), bf) for w in widths]
            + [vmem((2, 2, 2, 2, 2, 2, 16, w), bf) for w in widths]
            + [vmem((2, 4, 2, 2, 16, w), bf) for w in widths]
            + [
                vmem((2, 4, 2, 2, 2, 2, 2, 16, width), bf),
                vmem((4, 512, 128), f32),
                vmem((2, 4, 2, 8, 256), f32),
                vmem((2, 4, 2, 8, 256), f32),
                vmem((2, 4, 2, 8, 256), f32),
                vmem((4, 512, 128), f32),
                vmem((4, 512, 128), f32),
                vmem((2, 2, 16, 128), f32),
                vmem((6, 16, 128), f32),
                dma, dma, dma, dma((3, 2)), dma((3, 2)), dma((3, 2)),
                dma((3, 2, 2)), dma((3, 2, 2)), dma((3, 2, 2)),
                dma((3, 2, 4, 2)), dma((3, 4)), dma((3, 4)), dma((3, 2, 4)), dma((3, 2, 4)),
                dma((3, 4)), dma((3, 4)), dma((4,)), dma((4,)), dma, dma, dma,
            ],
            compiler_params=pltpu.CompilerParams(
                collective_id=0, has_side_effects=True, vmem_limit_bytes=56 * 1024 * 1024
            ),
        )(embeds, cluster_id, owner_slot)
        return both[0].reshape(1, 1, 3, 256), both[1].reshape(1, 1, 3, 256)

    return jax.shard_map(
        step,
        mesh=mesh,
        in_specs=(P(("group", "dev"), None), P(("group", "dev")), P()),
        out_specs=(P("group", "dev", None, None), P("group", "dev", None, None)),
        check_vma=False,
    )
```

```python
import functools
import math

import jax
import jax.numpy as jnp
from jax import lax
from jax.experimental import pallas as pl
from jax.experimental.pallas import tpu as pltpu
from jax.sharding import PartitionSpec as P

MESH = pl.DeviceIdType.MESH
SHARP = 20.0 * math.log2(math.e)
ABSENT = -1e30
COLS = ((0, 384), (384, 768), (768, 1024))
HALVES = 2


def mod4(value):
    return lax.rem(value + 16, 4)


def place():
    g = lax.axis_index("group")
    d = lax.axis_index("dev")
    return mod4(lax.rem(d, 4) + 3), mod4(g // 2 + 0), mod4(d // 4 + 1), lax.rem(g, 2)


def device(x, y, z, core):
    return (mod4(y - 0) * 2 + core, mod4(z - 1) * 4 + mod4(x - 3))


def root_of(g, l):
    y = g // 2
    if l < 2:
        x = lax.rem(g, 2) * 2 + l
        return x, y, mod4(x + y)
    x = mod4(y - lax.rem(g, 2))
    return x, y, mod4(x + y + 2)


def slot_positions(own):
    g = (own * 11) >> 5
    l = own - 3 * g
    y = g >> 1
    odd = g & 1
    second = l == 2
    x = jnp.where(second, (y - odd) & 3, odd * 2 + l)
    z = jnp.where(second, x + y + 2, x + y) & 3
    return (
        x * 6 + jnp.where(second, 4 + odd, y),
        y * 6 + jnp.where(second, 5 - odd, z),
        z * 6 + jnp.where(second, 4 + (x >> 1), x),
    )


class Order:
    def __init__(self, kind, x, y, z, core):
        self.kind = kind
        self.a, self.b, self.c = ((x, y, z), (y, z, x), (z, x, y))[kind]
        self.core = core

    def at(self, a, b, c):
        x, y, z = ((a, b, c), (c, a, b), (b, c, a))[self.kind]
        return device(x, y, z, self.core)

    def first(self, a, b):
        return mod4((a + b, b - a, a - b)[self.kind])

    def has_second(self, a, b):
        if self.kind == 0:
            return mod4(b - a) < 2
        if self.kind == 1:
            return mod4(b - 2 * a - 1) < 2
        return (a < 2) == (lax.rem(b, 2) == 1)

    def second_slot(self, a, b):
        return 4 + (mod4(b - a), mod4(b - 2 * a - 1), b // 2)[self.kind]


def kernel(
    embeds, cluster_id, owner_slot, both_out,
    raw, cid, owner, unit, pk0, pk1, pk2, ra0, ra1, ra2, rb0, rb1, rb2, rl0, rl1, rl2, rows, shade, veil, high, total, side_high, side_total, stats, landed,
    in_sem, id_sem, owner_sem, s1, r1, c1, s2, r2, c2, s3, r3, c3, s4, r4, sx, rx, sv, rv, so, ro, co,
):
    x, y, z, core = place()
    pk, ra, rb, rl = (pk0, pk1, pk2), (ra0, ra1, ra2), (rb0, rb1, rb2), (rl0, rl1, rl2)
    orders = [Order(kind, x, y, z, core) for kind in range(3)]
    is_first = z == mod4(x + y)
    is_second = (z == mod4(x + y + 2)) & (mod4(y - x) < 2)
    is_root = is_first | is_second
    root_g = jnp.where(is_first, 2 * y + x // 2, 2 * y + mod4(y - x))
    root_l = jnp.where(is_first, lax.rem(x, 2), 2)
    peer = device(x, y, z, 1 - core)
    g = lax.axis_index("group")

    barrier = pltpu.get_barrier_semaphore()

    def greet(target):
        pl.semaphore_signal(barrier, inc=1, device_id=target, device_id_type=MESH)

    for step in (1, 2, 3):
        greet(device(mod4(x + step), y, z, core))
        greet(device(x, mod4(y + step), z, core))
        greet(device(x, y, mod4(z + step), core))
    greet(peer)
    fetch = pltpu.make_async_copy(embeds, raw, in_sem)
    fetch_ids = pltpu.make_async_copy(cluster_id, cid, id_sem)
    fetch_owner = pltpu.make_async_copy(owner_slot, owner, owner_sem)
    fetch_ids.start()
    fetch_owner.start()
    fetch.start()

    n = raw.shape[0]
    fetch_ids.wait()
    fetch_owner.wait()
    ids = cid[...].reshape(1, n)
    own = jnp.zeros_like(ids)
    for c in range(24):
        own = jnp.where(ids == c, owner[c], own)
    member = (lax.broadcasted_iota(jnp.int32, (32, n), 0) == ids).astype(jnp.float32)
    earlier = lax.broadcasted_iota(jnp.int32, (n, n), 0) < lax.broadcasted_iota(jnp.int32, (n, n), 1)
    before = jnp.dot(
        member.astype(jnp.bfloat16), earlier.astype(jnp.float32).astype(jnp.bfloat16), preferred_element_type=jnp.float32
    )
    rank = jnp.sum(member * before, axis=0, keepdims=True).astype(jnp.int32)
    spots = [slot * 16 + (rank & 15) + (rank >> 4) * 384 for slot in slot_positions(own)]

    fetch.wait()
    wide = raw[...].astype(jnp.float32)
    scale = lax.rsqrt(jnp.sum(wide * wide, axis=1, keepdims=True) + 1e-6)
    unit[...] = (wide * scale).astype(jnp.bfloat16)

    targets = lax.broadcasted_iota(jnp.int32, (384, n), 0)
    for half in range(HALVES):
        for kind, (lo, hi) in enumerate(COLS):
            pick = (targets == spots[kind] - half * 384).astype(jnp.float32).astype(jnp.bfloat16)
            moved = jnp.dot(pick, unit[:, lo:hi], preferred_element_type=jnp.float32)
            pk[kind][half] = moved.astype(jnp.bfloat16).reshape(4, 6, 16, hi - lo)

    @pl.when(is_root)
    def _():
        high[...] = jnp.full(high.shape, ABSENT, jnp.float32)
        total[...] = jnp.zeros(total.shape, jnp.float32)
        side_high[...] = jnp.full(side_high.shape, ABSENT, jnp.float32)
        side_total[...] = jnp.zeros(side_total.shape, jnp.float32)

    pl.semaphore_wait(barrier, 10)

    def remote(src, dst, send, recv, target):
        return pltpu.make_async_remote_copy(
            src_ref=src, dst_ref=dst, send_sem=send, recv_sem=recv, device_id=target, device_id_type=MESH
        )

    def drain(ref, sem):
        pltpu.make_async_copy(ref, ref, sem).wait()

    def first_phase(half):
        for kind, order in enumerate(orders):
            a, b, c = order.a, order.b, order.c
            for step in (1, 2, 3):
                to = mod4(a + step)
                remote(
                    pk[kind].at[half, to], ra[kind].at[half, a // 2, lax.rem(a, 2)],
                    s1.at[kind, half], r1.at[kind, half], order.at(to, b, c),
                ).start()
            pltpu.make_async_copy(
                pk[kind].at[half, a], ra[kind].at[half, a // 2, lax.rem(a, 2)], c1.at[kind, half]
            ).start()

    def landing(kind, which, half, b):
        if kind == 2:
            return rb[kind].at[which, half, :, :, b // 2, lax.rem(b, 2)]
        return rb[kind].at[which, half, b // 2, lax.rem(b, 2)]

    def second_phase(half):
        for kind, order in enumerate(orders):
            a, b, c = order.a, order.b, order.c
            drain(pk[kind].at[half, pl.ds(0, 3)], r1.at[kind, half])
            drain(pk[kind].at[half, 0], c1.at[kind, half])
            for step in (1, 2, 3):
                to = mod4(b + step)
                remote(
                    ra[kind].at[half, :, :, to], landing(kind, 0, half, b),
                    s2.at[kind, half, 0], r2.at[kind, half, 0], order.at(a, to, c),
                ).start()

                @pl.when(order.has_second(a, to))
                def _():
                    remote(
                        ra[kind].at[half, :, :, order.second_slot(a, to)], landing(kind, 1, half, b),
                        s2.at[kind, half, 1], r2.at[kind, half, 1], order.at(a, to, c),
                    ).start()

            pltpu.make_async_copy(ra[kind].at[half, :, :, b], landing(kind, 0, half, b), c2.at[kind, half, 0]).start()

            @pl.when(order.has_second(a, b))
            def _():
                pltpu.make_async_copy(
                    ra[kind].at[half, :, :, order.second_slot(a, b)], landing(kind, 1, half, b), c2.at[kind, half, 1]
                ).start()

    def piece(kind, which, q, low, c):
        lo, hi = COLS[kind]
        half, odd = q // 2, q % 2
        cols = pl.ds(lo, hi - lo)
        cl, ch = lax.rem(c, 2), c // 2
        other = lax.rem(odd + cl + low, 2)
        if kind == 0:
            dst = rows.at[0, q, cl, ch, low, :, :, :, cols]
        elif kind == 1:
            dst = rows.at[0, q, low, :, other, :, ch, :, cols]
        else:
            dst = rows.at[0, q, low, :, cl, ch, :, :, cols]
        return rb[kind].at[which, half, :, low, :, other], dst

    def sends(kind, which):
        order = orders[kind]
        to = mod4(order.first(order.a, order.b) + 2 * which)
        return order.c != to, to

    def third_phase(q):
        half = q // 2
        for kind, order in enumerate(orders):
            a, b = order.a, order.b

            def pass_on(which):
                if q % 2 == 0:
                    drain(pk[kind].at[half, pl.ds(0, 2)], r2.at[kind, half, which])
                    drain(rb[kind].at[0, 0, 0, 0], c2.at[kind, half, which])
                away, to = sends(kind, which)
                far = order.c == mod4(to + 2)

                def pace(low):
                    if q:
                        @pl.when(jnp.logical_not(is_root))
                        def _():
                            drain(rb[kind].at[0, 0, 0, 0], s3.at[kind, which, q - 1, low])

                @pl.when(away & jnp.logical_not(far))
                def _():
                    for low in range(2):
                        pace(low)
                        src, dst = piece(kind, which, q, low, order.c)
                        remote(src, dst, s3.at[kind, which, q, low], r3.at[kind, q], order.at(a, b, to)).start()

                @pl.when(far)
                def _():
                    for low in range(2):
                        pace(low)
                        src, _ = piece(kind, which, q, low, order.c)
                        remote(
                            src, rl[kind].at[which, q], s3.at[kind, which, q, low], r4.at[kind, which, q],
                            order.at(a, b, mod4(order.c + 1 + 2 * low)),
                        ).start()

                @pl.when(jnp.logical_not(away))
                def _():
                    for low in range(2):
                        src, dst = piece(kind, which, q, low, order.c)
                        pltpu.make_async_copy(src, dst, c3.at[kind, q]).start()

            pass_on(0)

            @pl.when(order.has_second(a, b))
            def _():
                pass_on(1)

    def beside(kind, which):
        away, to = sends(kind, which)
        near = away & (orders[kind].c != mod4(to + 2))
        if which:
            near = near & orders[kind].has_second(orders[kind].a, orders[kind].b)
        return near, to

    def relay(q):
        for kind, order in enumerate(orders):
            for which in range(2):
                near, to = beside(kind, which)

                @pl.when(near)
                def _():
                    drain(rb[kind].at[0, 0, 0, 0], r4.at[kind, which, q])
                    low = jnp.where(order.c == mod4(to + 3), 0, 1)
                    _, dst = piece(kind, which, q, low, mod4(to + 2))
                    remote(
                        rl[kind].at[which, q], dst, s4.at[kind, which, q], r3.at[kind, q], order.at(order.a, order.b, to)
                    ).start()

    eye = lax.broadcasted_iota(jnp.int32, (256, 256), 0) == lax.broadcasted_iota(jnp.int32, (256, 256), 1)

    def block(which, q, part):
        return rows[which, q, part].reshape(256, 1024)

    def chunk(which, q):
        return rows[which, q].reshape(512, 1024)

    def scores(left, right):
        return lax.dot_general(left, right, (((1,), (1,)), ((), ())), preferred_element_type=jnp.float32)

    strip = 64

    def fold(values, merge):
        return merge(values.reshape(values.shape[0] // 8, 8, 128), axis=0)

    def merge_columns(which, q, part, tops, masses):
        for lane in range(2):
            cols = slice(lane * 128, lane * 128 + 128)
            high[which, q, part, :, cols] = jnp.maximum(high[which, q, part, :, cols], tops[lane])
            total[which, q, part, :, cols] = total[which, q, part, :, cols] + masses[lane]

    def both_ways(left, right, own_q, first, which, q, part):
        score = scores(left, right)
        tops, masses = [None, None], [None, None]
        for row in range(0, left.shape[0], strip):
            lines = slice(first + row, first + row + strip)
            row_veil = shade[own_q, lines]
            levels, powers = [], []
            for lane in range(2):
                cols = slice(lane * 128, lane * 128 + 128)
                level = score[row : row + strip, cols] * SHARP + (row_veil + veil[which, q, part, 0:1, cols])
                power = jnp.exp2(level)
                top, mass = fold(level, jnp.max), fold(power, jnp.sum)
                tops[lane] = top if row == 0 else jnp.maximum(tops[lane], top)
                masses[lane] = mass if row == 0 else masses[lane] + mass
                levels.append(level)
                powers.append(power)
            side_high[own_q, lines] = jnp.maximum(side_high[own_q, lines], jnp.maximum(levels[0], levels[1]))
            side_total[own_q, lines] = side_total[own_q, lines] + (powers[0] + powers[1])
        merge_columns(which, q, part, tops, masses)

    def own_pairs(q):
        me = chunk(0, q)
        score = [scores(me, block(0, q, part)) for part in range(2)]
        for part in range(2):
            square = jnp.where(eye, score[part][part * 256 : part * 256 + 256], 0.0)
            there = jnp.where(jnp.sum(square, axis=1, keepdims=True) > 0.5, 0.0, ABSENT)
            shade[q, part * 256 : part * 256 + 256] = jnp.broadcast_to(there, (256, 128))
            seen = jnp.sum(square, axis=0, keepdims=True) > 0.5
            veil[0, q, part] = jnp.broadcast_to(jnp.where(seen, -SHARP, ABSENT), (8, 256))
        remote(veil.at[0, q], veil.at[1, q], sv.at[q], rv.at[q], peer).start()
        for part in range(2):
            tops, masses = [None, None], [None, None]
            for row in range(0, 512, strip):
                for lane in range(2):
                    cols = slice(lane * 128, lane * 128 + 128)
                    level = score[part][row : row + strip, cols] * SHARP + (shade[q, row : row + strip] - SHARP)
                    if row // 256 == part:
                        level = jnp.where(eye[row % 256 : row % 256 + strip, cols], ABSENT, level)
                    top, mass = fold(level, jnp.max), fold(jnp.exp2(level), jnp.sum)
                    tops[lane] = top if row == 0 else jnp.maximum(tops[lane], top)
                    masses[lane] = mass if row == 0 else masses[lane] + mass
            merge_columns(0, q, part, tops, masses)
        for old in range(q):
            left = chunk(0, old)
            for part in range(2):
                both_ways(left, block(0, q, part), old, 0, 0, q, part)

    def cross_pairs(q):
        for mine in range(2):
            part = lax.rem(mine + core, 2)
            both_ways(
                block(0, q, mine), block(1, q, part), q, mine * 256, 1, q, part
            )
        for old in range(q):
            left = chunk(0, old)
            for part in range(2):
                both_ways(left, block(1, q, part), old, 0, 1, q, part)

    def arrive(q):
        for kind in range(3):
            drain(pk[kind].at[0], r3.at[kind, q])
            drain(rb[kind].at[0, 0, 0], c3.at[kind, q])
            lo, hi = COLS[kind]
            cols = pl.ds(lo, hi - lo)
            remote(
                rows.at[0, q, :, :, :, :, :, :, cols], rows.at[1, q, :, :, :, :, :, :, cols],
                sx.at[kind, q], rx.at[kind, q], peer,
            ).start()

    def process(q):
        if q not in (2, 3):
            arrive(q)
        own_pairs(q)
        for kind in range(3):
            drain(rb[kind].at[0], rx.at[kind, q])
        drain(veil.at[1, q], rv.at[q])
        if q + 1 in (2, 3):
            arrive(q + 1)
        cross_pairs(q)

    first_phase(0)
    first_phase(1)
    second_phase(0)
    second_phase(1)
    third_phase(0)
    relay(0)
    third_phase(1)
    relay(1)
    third_phase(2)
    relay(2)
    third_phase(3)
    relay(3)

    @pl.when(is_root)
    def _():
        process(0)


    @pl.when(is_root)
    def _():
        process(1)


    @pl.when(is_root)
    def _():
        process(2)


    @pl.when(is_root)
    def _():
        process(3)
        for q in range(4):
            for part in range(2):
                lines = slice(part * 256, part * 256 + 256)
                side = jnp.max(side_high[q, lines].T.reshape(16, 8, 256), axis=0)
                top = jnp.max(jnp.maximum(high[0, q, part], side), axis=0, keepdims=True)
                top = jnp.where(veil[0, q, part, 0:1] > 0.5 * ABSENT, top, -ABSENT)
                side = jnp.sum(side_total[q, lines].T.reshape(16, 8, 256), axis=0)
                mass = jnp.sum(total[0, q, part] + side, axis=0, keepdims=True)
                far_top = jnp.max(high[1, q, part], axis=0, keepdims=True)
                far_mass = jnp.sum(total[1, q, part], axis=0, keepdims=True)
                for line, value in ((q, top), (4 + q, mass), (8 + q, far_top), (12 + q, far_mass)):
                    for lane in range(2):
                        stats[part, lane, line : line + 1] = value[:, lane * 128 : lane * 128 + 128]
        spot = root_l * 2 + core
        for step in range(16):
            row, column = (1 + step // 4) % 4, (3 + step) % 4
            target = device(column, y, row, lax.rem(root_g, 2))
            src = stats.at[row % 2, row // 2]
            same = (x == column) & (z == row) & (core == lax.rem(root_g, 2))

            @pl.when(jnp.logical_not(same))
            def _():
                remote(src, landed.at[spot], so, ro, target).start()

            @pl.when(same)
            def _():
                copy = pltpu.make_async_copy(src, landed.at[spot], co)
                copy.start()
                copy.wait()

    for half in range(HALVES):
        for kind, order in enumerate(orders):
            a, b, c = order.a, order.b, order.c
            drain(pk[kind].at[half, pl.ds(0, 3)], s1.at[kind, half])
            drain(pk[kind].at[half, pl.ds(0, 2)], s2.at[kind, half, 0])
            for step in (1, 2, 3):
                @pl.when(order.has_second(a, mod4(b + step)))
                def _():
                    drain(rb[kind].at[0, 0, 0, 0], s2.at[kind, half, 1])

    for kind in range(3):
        for which in range(2):
            near, _ = beside(kind, which)

            @pl.when(near)
            def _():
                for q in range(4):
                    drain(rb[kind].at[0, 0, 0, 0], s4.at[kind, which, q])

    for kind, order in enumerate(orders):
        for which in range(2):
            away, _ = sends(kind, which)
            if which:
                away = away & order.has_second(order.a, order.b)

            @pl.when(away)
            def _():
                for low in range(2):
                    drain(rb[kind].at[0, 0, 0, 0], s3.at[kind, which, 3, low])

                @pl.when(is_root)
                def _():
                    for q in range(3):
                        for low in range(2):
                            drain(rb[kind].at[0, 0, 0, 0], s3.at[kind, which, q, low])

    @pl.when(is_root)
    def _():
        for q in range(4):
            for kind in range(3):
                drain(rb[kind].at[0], sx.at[kind, q])
            drain(veil.at[0, q], sv.at[q])
        for count in range(15):
            drain(stats.at[0, 0], so)

        @pl.when(core != lax.rem(root_g, 2))
        def _():
            drain(stats.at[0, 0], so)

    in_mine = jnp.int32(0)
    for l in range(3):
        qx, qy, qz = root_of(g, l)
        in_mine = in_mine + jnp.where((qx == x) & (qy == y) & (qz == z), 1, 0)

    @pl.when(in_mine == 0)
    def _():
        drain(landed, ro)

    @pl.when(in_mine != 0)
    def _():
        drain(landed.at[pl.ds(0, 5)], ro)

    lane = lax.broadcasted_iota(jnp.int32, (48, 128), 1)
    first = lax.broadcasted_iota(jnp.int32, (8, 128), 0) < 4
    final = []
    for l in range(3):
        for k in range(2):
            mine, other = landed[2 * l + k], landed[2 * l + 1 - k]
            top = jnp.maximum(mine[0:4], other[8:12])
            mass = mine[4:8] + other[12:16]
            top = jnp.concatenate([top, top], axis=0)
            mass = jnp.concatenate([mass, mass], axis=0)
            paired = top > 0.5 * ABSENT
            near_row = jnp.where(paired, top * (1.0 / SHARP) + 1.0, -2.0)
            lse_row = jnp.where(paired, 20.0 + jnp.log(jnp.where(paired, mass, 1.0)), 0.0)
            final.append(jnp.where(top > -0.5 * ABSENT, 0.0, jnp.where(first, near_row, lse_row)))
    held = jnp.concatenate(final, axis=0)
    out = [[jnp.zeros((1, 128), jnp.float32) for _ in range(6)] for _ in range(2)]
    for yh in range(2):
        turned = pltpu.roll(held, lax.rem(256 - yh * 32 - (x // 2) * 16, 128), 1)
        for odd in range(2):
            start = lax.rem(odd + z + x, 2) * 64
            kept = jnp.where((lane >= start) & (lane < start + 16), turned, 0.0)
            for k in range(2):
                for half in range(HALVES):
                    shift = k * 32 + half * 16
                    moved = pltpu.roll(kept, shift, 1) if shift else kept
                    for l in range(3):
                        line = (2 * l + k) * 8 + half * 2 + odd
                        out[yh][l] = out[yh][l] + moved[line : line + 1]
                        out[yh][3 + l] = out[yh][3 + l] + moved[line + 4 : line + 5]
        for which in range(2):
            for l in range(3):
                both_out[which, l, :, yh * 128 : yh * 128 + 128] = out[yh][3 * which + l]


def solution(mesh):
    def step(embeds, cluster_id, owner_slot):
        n, width = embeds.shape
        bf, f32 = jnp.bfloat16, jnp.float32
        widths = [hi - lo for lo, hi in COLS]
        vmem = pltpu.VMEM
        dma = pltpu.SemaphoreType.DMA
        both = pl.pallas_call(
            kernel,
            out_shape=jax.ShapeDtypeStruct((2, 3, 1, 256), f32),
            in_specs=[pl.BlockSpec(memory_space=pl.ANY)] * 3,
            out_specs=pl.BlockSpec(memory_space=pltpu.VMEM),
            scratch_shapes=[vmem((n, width), bf), vmem((n,), jnp.int32), pltpu.SMEM((24,), jnp.int32), vmem((n, width), bf)]
            + [vmem((2, 4, 6, 16, w), bf) for w in widths]
            + [vmem((2, 2, 2, 6, 16, w), bf) for w in widths]
            + [vmem((2, 2, 2, 2, 2, 2, 16, w), bf) for w in widths]
            + [vmem((2, 4, 2, 2, 16, w), bf) for w in widths]
            + [
                vmem((2, 4, 2, 2, 2, 2, 2, 16, width), bf),
                vmem((4, 512, 128), f32),
                vmem((2, 4, 2, 8, 256), f32),
                vmem((2, 4, 2, 8, 256), f32),
                vmem((2, 4, 2, 8, 256), f32),
                vmem((4, 512, 128), f32),
                vmem((4, 512, 128), f32),
                vmem((2, 2, 16, 128), f32),
                vmem((6, 16, 128), f32),
                dma, dma, dma, dma((3, 2)), dma((3, 2)), dma((3, 2)),
                dma((3, 2, 2)), dma((3, 2, 2)), dma((3, 2, 2)),
                dma((3, 2, 4, 2)), dma((3, 4)), dma((3, 4)), dma((3, 2, 4)), dma((3, 2, 4)),
                dma((3, 4)), dma((3, 4)), dma((4,)), dma((4,)), dma, dma, dma,
            ],
            compiler_params=pltpu.CompilerParams(
                collective_id=0, has_side_effects=True, vmem_limit_bytes=56 * 1024 * 1024
            ),
        )(embeds, cluster_id, owner_slot)
        return both[0].reshape(1, 1, 3, 256), both[1].reshape(1, 1, 3, 256)

    return jax.shard_map(
        step,
        mesh=mesh,
        in_specs=(P(("group", "dev"), None), P(("group", "dev")), P()),
        out_specs=(P("group", "dev", None, None), P("group", "dev", None, None)),
        check_vma=False,
    )
```

```python
import functools
import math

import jax
import jax.numpy as jnp
from jax import lax
from jax.experimental import pallas as pl
from jax.experimental.pallas import tpu as pltpu
from jax.sharding import PartitionSpec as P

MESH = pl.DeviceIdType.MESH
SHARP = 20.0 * math.log2(math.e)
ABSENT = -1e30
COLS = ((0, 256), (256, 640), (640, 1024))
HALVES = 2


def mod4(value):
    return lax.rem(value + 16, 4)


def place():
    g = lax.axis_index("group")
    d = lax.axis_index("dev")
    return mod4(lax.rem(d, 4) + 3), mod4(g // 2 + 0), mod4(d // 4 + 1), lax.rem(g, 2)


def device(x, y, z, core):
    return (mod4(y - 0) * 2 + core, mod4(z - 1) * 4 + mod4(x - 3))


def root_of(g, l):
    y = g // 2
    if l < 2:
        x = lax.rem(g, 2) * 2 + l
        return x, y, mod4(x + y)
    x = mod4(y - lax.rem(g, 2))
    return x, y, mod4(x + y + 2)


def slot_positions(own):
    g = (own * 11) >> 5
    l = own - 3 * g
    y = g >> 1
    odd = g & 1
    second = l == 2
    x = jnp.where(second, (y - odd) & 3, odd * 2 + l)
    z = jnp.where(second, x + y + 2, x + y) & 3
    return (
        x * 6 + jnp.where(second, 4 + odd, y),
        y * 6 + jnp.where(second, 5 - odd, z),
        z * 6 + jnp.where(second, 4 + (x >> 1), x),
    )


class Order:
    def __init__(self, kind, x, y, z, core):
        self.kind = kind
        self.a, self.b, self.c = ((x, y, z), (y, z, x), (z, x, y))[kind]
        self.core = core

    def at(self, a, b, c):
        x, y, z = ((a, b, c), (c, a, b), (b, c, a))[self.kind]
        return device(x, y, z, self.core)

    def first(self, a, b):
        return mod4((a + b, b - a, a - b)[self.kind])

    def has_second(self, a, b):
        if self.kind == 0:
            return mod4(b - a) < 2
        if self.kind == 1:
            return mod4(b - 2 * a - 1) < 2
        return (a < 2) == (lax.rem(b, 2) == 1)

    def second_slot(self, a, b):
        return 4 + (mod4(b - a), mod4(b - 2 * a - 1), b // 2)[self.kind]


def kernel(
    embeds, cluster_id, owner_slot, both_out,
    raw, cid, owner, unit, pk0, pk1, pk2, ra0, ra1, ra2, rb0, rb1, rb2, rl0, rl1, rl2, rows, shade, veil, high, total, side_high, side_total, stats, landed,
    in_sem, id_sem, owner_sem, s1, r1, c1, s2, r2, c2, s3, r3, c3, s4, r4, sx, rx, sv, rv, so, ro, co,
):
    x, y, z, core = place()
    pk, ra, rb, rl = (pk0, pk1, pk2), (ra0, ra1, ra2), (rb0, rb1, rb2), (rl0, rl1, rl2)
    orders = [Order(kind, x, y, z, core) for kind in range(3)]
    is_first = z == mod4(x + y)
    is_second = (z == mod4(x + y + 2)) & (mod4(y - x) < 2)
    is_root = is_first | is_second
    root_g = jnp.where(is_first, 2 * y + x // 2, 2 * y + mod4(y - x))
    root_l = jnp.where(is_first, lax.rem(x, 2), 2)
    peer = device(x, y, z, 1 - core)
    g = lax.axis_index("group")

    barrier = pltpu.get_barrier_semaphore()

    def greet(target):
        pl.semaphore_signal(barrier, inc=1, device_id=target, device_id_type=MESH)

    for step in (1, 2, 3):
        greet(device(mod4(x + step), y, z, core))
        greet(device(x, mod4(y + step), z, core))
        greet(device(x, y, mod4(z + step), core))
    greet(peer)
    fetch = pltpu.make_async_copy(embeds, raw, in_sem)
    fetch_ids = pltpu.make_async_copy(cluster_id, cid, id_sem)
    fetch_owner = pltpu.make_async_copy(owner_slot, owner, owner_sem)
    fetch_ids.start()
    fetch_owner.start()
    fetch.start()

    n = raw.shape[0]
    fetch_ids.wait()
    fetch_owner.wait()
    ids = cid[...].reshape(1, n)
    own = jnp.zeros_like(ids)
    for c in range(24):
        own = jnp.where(ids == c, owner[c], own)
    member = (lax.broadcasted_iota(jnp.int32, (32, n), 0) == ids).astype(jnp.float32)
    earlier = lax.broadcasted_iota(jnp.int32, (n, n), 0) < lax.broadcasted_iota(jnp.int32, (n, n), 1)
    before = jnp.dot(
        member.astype(jnp.bfloat16), earlier.astype(jnp.float32).astype(jnp.bfloat16), preferred_element_type=jnp.float32
    )
    rank = jnp.sum(member * before, axis=0, keepdims=True).astype(jnp.int32)
    spots = [slot * 16 + (rank & 15) + (rank >> 4) * 384 for slot in slot_positions(own)]

    fetch.wait()
    wide = raw[...].astype(jnp.float32)
    scale = lax.rsqrt(jnp.sum(wide * wide, axis=1, keepdims=True) + 1e-6)
    unit[...] = (wide * scale).astype(jnp.bfloat16)

    targets = lax.broadcasted_iota(jnp.int32, (384, n), 0)
    for half in range(HALVES):
        for kind, (lo, hi) in enumerate(COLS):
            pick = (targets == spots[kind] - half * 384).astype(jnp.float32).astype(jnp.bfloat16)
            moved = jnp.dot(pick, unit[:, lo:hi], preferred_element_type=jnp.float32)
            pk[kind][half] = moved.astype(jnp.bfloat16).reshape(4, 6, 16, hi - lo)

    @pl.when(is_root)
    def _():
        high[...] = jnp.full(high.shape, ABSENT, jnp.float32)
        total[...] = jnp.zeros(total.shape, jnp.float32)
        side_high[...] = jnp.full(side_high.shape, ABSENT, jnp.float32)
        side_total[...] = jnp.zeros(side_total.shape, jnp.float32)

    pl.semaphore_wait(barrier, 10)

    def remote(src, dst, send, recv, target):
        return pltpu.make_async_remote_copy(
            src_ref=src, dst_ref=dst, send_sem=send, recv_sem=recv, device_id=target, device_id_type=MESH
        )

    def drain(ref, sem):
        pltpu.make_async_copy(ref, ref, sem).wait()

    def first_phase(half):
        for kind, order in enumerate(orders):
            a, b, c = order.a, order.b, order.c
            for step in (1, 2, 3):
                to = mod4(a + step)
                remote(
                    pk[kind].at[half, to], ra[kind].at[half, a // 2, lax.rem(a, 2)],
                    s1.at[kind, half], r1.at[kind, half], order.at(to, b, c),
                ).start()
            pltpu.make_async_copy(
                pk[kind].at[half, a], ra[kind].at[half, a // 2, lax.rem(a, 2)], c1.at[kind, half]
            ).start()

    def landing(kind, which, half, b):
        if kind == 2:
            return rb[kind].at[which, half, :, :, b // 2, lax.rem(b, 2)]
        return rb[kind].at[which, half, b // 2, lax.rem(b, 2)]

    def second_phase(half):
        for kind, order in enumerate(orders):
            a, b, c = order.a, order.b, order.c
            drain(pk[kind].at[half, pl.ds(0, 3)], r1.at[kind, half])
            drain(pk[kind].at[half, 0], c1.at[kind, half])
            for step in (1, 2, 3):
                to = mod4(b + step)
                remote(
                    ra[kind].at[half, :, :, to], landing(kind, 0, half, b),
                    s2.at[kind, half, 0], r2.at[kind, half, 0], order.at(a, to, c),
                ).start()

                @pl.when(order.has_second(a, to))
                def _():
                    remote(
                        ra[kind].at[half, :, :, order.second_slot(a, to)], landing(kind, 1, half, b),
                        s2.at[kind, half, 1], r2.at[kind, half, 1], order.at(a, to, c),
                    ).start()

            pltpu.make_async_copy(ra[kind].at[half, :, :, b], landing(kind, 0, half, b), c2.at[kind, half, 0]).start()

            @pl.when(order.has_second(a, b))
            def _():
                pltpu.make_async_copy(
                    ra[kind].at[half, :, :, order.second_slot(a, b)], landing(kind, 1, half, b), c2.at[kind, half, 1]
                ).start()

    def piece(kind, which, q, low, c):
        lo, hi = COLS[kind]
        half, odd = q // 2, q % 2
        cols = pl.ds(lo, hi - lo)
        cl, ch = lax.rem(c, 2), c // 2
        other = lax.rem(odd + cl + low, 2)
        if kind == 0:
            dst = rows.at[0, q, cl, ch, low, :, :, :, cols]
        elif kind == 1:
            dst = rows.at[0, q, low, :, other, :, ch, :, cols]
        else:
            dst = rows.at[0, q, low, :, cl, ch, :, :, cols]
        return rb[kind].at[which, half, :, low, :, other], dst

    def sends(kind, which):
        order = orders[kind]
        to = mod4(order.first(order.a, order.b) + 2 * which)
        return order.c != to, to

    def third_phase(q):
        half = q // 2
        for kind, order in enumerate(orders):
            a, b = order.a, order.b

            def pass_on(which):
                if q % 2 == 0:
                    drain(pk[kind].at[half, pl.ds(0, 2)], r2.at[kind, half, which])
                    drain(rb[kind].at[0, 0, 0, 0], c2.at[kind, half, which])
                away, to = sends(kind, which)
                far = order.c == mod4(to + 2)

                def pace(low):
                    if q:
                        @pl.when(jnp.logical_not(is_root))
                        def _():
                            drain(rb[kind].at[0, 0, 0, 0], s3.at[kind, which, q - 1, low])

                @pl.when(away & jnp.logical_not(far))
                def _():
                    for low in range(2):
                        pace(low)
                        src, dst = piece(kind, which, q, low, order.c)
                        remote(src, dst, s3.at[kind, which, q, low], r3.at[kind, q], order.at(a, b, to)).start()

                @pl.when(far)
                def _():
                    for low in range(2):
                        pace(low)
                        src, _ = piece(kind, which, q, low, order.c)
                        remote(
                            src, rl[kind].at[which, q], s3.at[kind, which, q, low], r4.at[kind, which, q],
                            order.at(a, b, mod4(order.c + 1 + 2 * low)),
                        ).start()

                @pl.when(jnp.logical_not(away))
                def _():
                    for low in range(2):
                        src, dst = piece(kind, which, q, low, order.c)
                        pltpu.make_async_copy(src, dst, c3.at[kind, q]).start()

            pass_on(0)

            @pl.when(order.has_second(a, b))
            def _():
                pass_on(1)

    def beside(kind, which):
        away, to = sends(kind, which)
        near = away & (orders[kind].c != mod4(to + 2))
        if which:
            near = near & orders[kind].has_second(orders[kind].a, orders[kind].b)
        return near, to

    def relay(q):
        for kind, order in enumerate(orders):
            for which in range(2):
                near, to = beside(kind, which)

                @pl.when(near)
                def _():
                    drain(rb[kind].at[0, 0, 0, 0], r4.at[kind, which, q])
                    low = jnp.where(order.c == mod4(to + 3), 0, 1)
                    _, dst = piece(kind, which, q, low, mod4(to + 2))
                    remote(
                        rl[kind].at[which, q], dst, s4.at[kind, which, q], r3.at[kind, q], order.at(order.a, order.b, to)
                    ).start()

    eye = lax.broadcasted_iota(jnp.int32, (256, 256), 0) == lax.broadcasted_iota(jnp.int32, (256, 256), 1)

    def block(which, q, part):
        return rows[which, q, part].reshape(256, 1024)

    def chunk(which, q):
        return rows[which, q].reshape(512, 1024)

    def scores(left, right):
        return lax.dot_general(left, right, (((1,), (1,)), ((), ())), preferred_element_type=jnp.float32)

    strip = 64

    def fold(values, merge):
        return merge(values.reshape(values.shape[0] // 8, 8, 128), axis=0)

    def merge_columns(which, q, part, tops, masses):
        for lane in range(2):
            cols = slice(lane * 128, lane * 128 + 128)
            high[which, q, part, :, cols] = jnp.maximum(high[which, q, part, :, cols], tops[lane])
            total[which, q, part, :, cols] = total[which, q, part, :, cols] + masses[lane]

    def both_ways(left, right, own_q, first, which, q, part):
        score = scores(left, right)
        tops, masses = [None, None], [None, None]
        for row in range(0, left.shape[0], strip):
            lines = slice(first + row, first + row + strip)
            row_veil = shade[own_q, lines]
            levels, powers = [], []
            for lane in range(2):
                cols = slice(lane * 128, lane * 128 + 128)
                level = score[row : row + strip, cols] * SHARP + (row_veil + veil[which, q, part, 0:1, cols])
                power = jnp.exp2(level)
                top, mass = fold(level, jnp.max), fold(power, jnp.sum)
                tops[lane] = top if row == 0 else jnp.maximum(tops[lane], top)
                masses[lane] = mass if row == 0 else masses[lane] + mass
                levels.append(level)
                powers.append(power)
            side_high[own_q, lines] = jnp.maximum(side_high[own_q, lines], jnp.maximum(levels[0], levels[1]))
            side_total[own_q, lines] = side_total[own_q, lines] + (powers[0] + powers[1])
        merge_columns(which, q, part, tops, masses)

    def own_pairs(q):
        me = chunk(0, q)
        score = [scores(me, block(0, q, part)) for part in range(2)]
        for part in range(2):
            square = jnp.where(eye, score[part][part * 256 : part * 256 + 256], 0.0)
            there = jnp.where(jnp.sum(square, axis=1, keepdims=True) > 0.5, 0.0, ABSENT)
            shade[q, part * 256 : part * 256 + 256] = jnp.broadcast_to(there, (256, 128))
            seen = jnp.sum(square, axis=0, keepdims=True) > 0.5
            veil[0, q, part] = jnp.broadcast_to(jnp.where(seen, -SHARP, ABSENT), (8, 256))
        remote(veil.at[0, q], veil.at[1, q], sv.at[q], rv.at[q], peer).start()
        for part in range(2):
            tops, masses = [None, None], [None, None]
            for row in range(0, 512, strip):
                for lane in range(2):
                    cols = slice(lane * 128, lane * 128 + 128)
                    level = score[part][row : row + strip, cols] * SHARP + (shade[q, row : row + strip] - SHARP)
                    if row // 256 == part:
                        level = jnp.where(eye[row % 256 : row % 256 + strip, cols], ABSENT, level)
                    top, mass = fold(level, jnp.max), fold(jnp.exp2(level), jnp.sum)
                    tops[lane] = top if row == 0 else jnp.maximum(tops[lane], top)
                    masses[lane] = mass if row == 0 else masses[lane] + mass
            merge_columns(0, q, part, tops, masses)
        for old in range(q):
            left = chunk(0, old)
            for part in range(2):
                both_ways(left, block(0, q, part), old, 0, 0, q, part)

    def cross_pairs(q):
        for mine in range(2):
            part = lax.rem(mine + core, 2)
            both_ways(
                block(0, q, mine), block(1, q, part), q, mine * 256, 1, q, part
            )
        for old in range(q):
            left = chunk(0, old)
            for part in range(2):
                both_ways(left, block(1, q, part), old, 0, 1, q, part)

    def arrive(q):
        for kind in range(3):
            drain(pk[kind].at[0], r3.at[kind, q])
            drain(rb[kind].at[0, 0, 0], c3.at[kind, q])
            lo, hi = COLS[kind]
            cols = pl.ds(lo, hi - lo)
            remote(
                rows.at[0, q, :, :, :, :, :, :, cols], rows.at[1, q, :, :, :, :, :, :, cols],
                sx.at[kind, q], rx.at[kind, q], peer,
            ).start()

    def process(q):
        if q not in (2, 3):
            arrive(q)
        own_pairs(q)
        for kind in range(3):
            drain(rb[kind].at[0], rx.at[kind, q])
        drain(veil.at[1, q], rv.at[q])
        if q + 1 in (2, 3):
            arrive(q + 1)
        cross_pairs(q)

    first_phase(0)
    first_phase(1)
    second_phase(0)
    second_phase(1)
    third_phase(0)
    relay(0)
    third_phase(1)
    relay(1)
    third_phase(2)
    relay(2)
    third_phase(3)
    relay(3)

    @pl.when(is_root)
    def _():
        process(0)


    @pl.when(is_root)
    def _():
        process(1)


    @pl.when(is_root)
    def _():
        process(2)


    @pl.when(is_root)
    def _():
        process(3)
        for q in range(4):
            for part in range(2):
                lines = slice(part * 256, part * 256 + 256)
                side = jnp.max(side_high[q, lines].T.reshape(16, 8, 256), axis=0)
                top = jnp.max(jnp.maximum(high[0, q, part], side), axis=0, keepdims=True)
                top = jnp.where(veil[0, q, part, 0:1] > 0.5 * ABSENT, top, -ABSENT)
                side = jnp.sum(side_total[q, lines].T.reshape(16, 8, 256), axis=0)
                mass = jnp.sum(total[0, q, part] + side, axis=0, keepdims=True)
                far_top = jnp.max(high[1, q, part], axis=0, keepdims=True)
                far_mass = jnp.sum(total[1, q, part], axis=0, keepdims=True)
                for line, value in ((q, top), (4 + q, mass), (8 + q, far_top), (12 + q, far_mass)):
                    for lane in range(2):
                        stats[part, lane, line : line + 1] = value[:, lane * 128 : lane * 128 + 128]
        spot = root_l * 2 + core
        for step in range(16):
            row, column = (1 + step // 4) % 4, (3 + step) % 4
            target = device(column, y, row, lax.rem(root_g, 2))
            src = stats.at[row % 2, row // 2]
            same = (x == column) & (z == row) & (core == lax.rem(root_g, 2))

            @pl.when(jnp.logical_not(same))
            def _():
                remote(src, landed.at[spot], so, ro, target).start()

            @pl.when(same)
            def _():
                copy = pltpu.make_async_copy(src, landed.at[spot], co)
                copy.start()
                copy.wait()

    for half in range(HALVES):
        for kind, order in enumerate(orders):
            a, b, c = order.a, order.b, order.c
            drain(pk[kind].at[half, pl.ds(0, 3)], s1.at[kind, half])
            drain(pk[kind].at[half, pl.ds(0, 2)], s2.at[kind, half, 0])
            for step in (1, 2, 3):
                @pl.when(order.has_second(a, mod4(b + step)))
                def _():
                    drain(rb[kind].at[0, 0, 0, 0], s2.at[kind, half, 1])

    for kind in range(3):
        for which in range(2):
            near, _ = beside(kind, which)

            @pl.when(near)
            def _():
                for q in range(4):
                    drain(rb[kind].at[0, 0, 0, 0], s4.at[kind, which, q])

    for kind, order in enumerate(orders):
        for which in range(2):
            away, _ = sends(kind, which)
            if which:
                away = away & order.has_second(order.a, order.b)

            @pl.when(away)
            def _():
                for low in range(2):
                    drain(rb[kind].at[0, 0, 0, 0], s3.at[kind, which, 3, low])

                @pl.when(is_root)
                def _():
                    for q in range(3):
                        for low in range(2):
                            drain(rb[kind].at[0, 0, 0, 0], s3.at[kind, which, q, low])

    @pl.when(is_root)
    def _():
        for q in range(4):
            for kind in range(3):
                drain(rb[kind].at[0], sx.at[kind, q])
            drain(veil.at[0, q], sv.at[q])
        for count in range(15):
            drain(stats.at[0, 0], so)

        @pl.when(core != lax.rem(root_g, 2))
        def _():
            drain(stats.at[0, 0], so)

    in_mine = jnp.int32(0)
    for l in range(3):
        qx, qy, qz = root_of(g, l)
        in_mine = in_mine + jnp.where((qx == x) & (qy == y) & (qz == z), 1, 0)

    @pl.when(in_mine == 0)
    def _():
        drain(landed, ro)

    @pl.when(in_mine != 0)
    def _():
        drain(landed.at[pl.ds(0, 5)], ro)

    lane = lax.broadcasted_iota(jnp.int32, (48, 128), 1)
    first = lax.broadcasted_iota(jnp.int32, (8, 128), 0) < 4
    final = []
    for l in range(3):
        for k in range(2):
            mine, other = landed[2 * l + k], landed[2 * l + 1 - k]
            top = jnp.maximum(mine[0:4], other[8:12])
            mass = mine[4:8] + other[12:16]
            top = jnp.concatenate([top, top], axis=0)
            mass = jnp.concatenate([mass, mass], axis=0)
            paired = top > 0.5 * ABSENT
            near_row = jnp.where(paired, top * (1.0 / SHARP) + 1.0, -2.0)
            lse_row = jnp.where(paired, 20.0 + jnp.log(jnp.where(paired, mass, 1.0)), 0.0)
            final.append(jnp.where(top > -0.5 * ABSENT, 0.0, jnp.where(first, near_row, lse_row)))
    held = jnp.concatenate(final, axis=0)
    out = [[jnp.zeros((1, 128), jnp.float32) for _ in range(6)] for _ in range(2)]
    for yh in range(2):
        turned = pltpu.roll(held, lax.rem(256 - yh * 32 - (x // 2) * 16, 128), 1)
        for odd in range(2):
            start = lax.rem(odd + z + x, 2) * 64
            kept = jnp.where((lane >= start) & (lane < start + 16), turned, 0.0)
            for k in range(2):
                for half in range(HALVES):
                    shift = k * 32 + half * 16
                    moved = pltpu.roll(kept, shift, 1) if shift else kept
                    for l in range(3):
                        line = (2 * l + k) * 8 + half * 2 + odd
                        out[yh][l] = out[yh][l] + moved[line : line + 1]
                        out[yh][3 + l] = out[yh][3 + l] + moved[line + 4 : line + 5]
        for which in range(2):
            for l in range(3):
                both_out[which, l, :, yh * 128 : yh * 128 + 128] = out[yh][3 * which + l]


def solution(mesh):
    def step(embeds, cluster_id, owner_slot):
        n, width = embeds.shape
        bf, f32 = jnp.bfloat16, jnp.float32
        widths = [hi - lo for lo, hi in COLS]
        vmem = pltpu.VMEM
        dma = pltpu.SemaphoreType.DMA
        both = pl.pallas_call(
            kernel,
            out_shape=jax.ShapeDtypeStruct((2, 3, 1, 256), f32),
            in_specs=[pl.BlockSpec(memory_space=pl.ANY)] * 3,
            out_specs=pl.BlockSpec(memory_space=pltpu.VMEM),
            scratch_shapes=[vmem((n, width), bf), vmem((n,), jnp.int32), pltpu.SMEM((24,), jnp.int32), vmem((n, width), bf)]
            + [vmem((2, 4, 6, 16, w), bf) for w in widths]
            + [vmem((2, 2, 2, 6, 16, w), bf) for w in widths]
            + [vmem((2, 2, 2, 2, 2, 2, 16, w), bf) for w in widths]
            + [vmem((2, 4, 2, 2, 16, w), bf) for w in widths]
            + [
                vmem((2, 4, 2, 2, 2, 2, 2, 16, width), bf),
                vmem((4, 512, 128), f32),
                vmem((2, 4, 2, 8, 256), f32),
                vmem((2, 4, 2, 8, 256), f32),
                vmem((2, 4, 2, 8, 256), f32),
                vmem((4, 512, 128), f32),
                vmem((4, 512, 128), f32),
                vmem((2, 2, 16, 128), f32),
                vmem((6, 16, 128), f32),
                dma, dma, dma, dma((3, 2)), dma((3, 2)), dma((3, 2)),
                dma((3, 2, 2)), dma((3, 2, 2)), dma((3, 2, 2)),
                dma((3, 2, 4, 2)), dma((3, 4)), dma((3, 4)), dma((3, 2, 4)), dma((3, 2, 4)),
                dma((3, 4)), dma((3, 4)), dma((4,)), dma((4,)), dma, dma, dma,
            ],
            compiler_params=pltpu.CompilerParams(
                collective_id=0, has_side_effects=True, vmem_limit_bytes=56 * 1024 * 1024
            ),
        )(embeds, cluster_id, owner_slot)
        return both[0].reshape(1, 1, 3, 256), both[1].reshape(1, 1, 3, 256)

    return jax.shard_map(
        step,
        mesh=mesh,
        in_specs=(P(("group", "dev"), None), P(("group", "dev")), P()),
        out_specs=(P("group", "dev", None, None), P("group", "dev", None, None)),
        check_vma=False,
    )
```
